256 devices in a mesh: lat: 8 (over x, core), lon: 16 (over y_hi, z), section: 2 (over y_lo).
Axes of the slice: x: 4, y: 4 (y_hi: 2, y_lo: 2; y = y_hi * 2 + y_lo), z: 8, core: 2. Of those that a mesh axis runs over, the one named last changes fastest.
Arguments:
- fields: bfloat16 [4, 69, 512, 1024], P(None, None, 'lat', 'lon'), may hold values from -6 to 6
- embed_weight: bfloat16 [10, 10, 69, 1024], P('section'), may hold values from -0.078125 to 0.078125
- embed_bias: bfloat16 [1024], replicated, may hold values from -3 to 3
- pos_embed: bfloat16 [64, 128, 1024], P('lat', 'lon'), may hold values from -6 to 6
- member_ids: int32 [4], P('section'), may hold values from 0 to 49
- member_table: bfloat16 [50, 1024], replicated, may hold values from -6 to 6
- norm_gain: float32 [1024], replicated, may hold values from 0.5 to 1.5
- w_qkv: bfloat16 [3, 1024, 1024], P(None, 'lon'), may hold values from -0.1875 to 0.1875
- query_gain: float32 [16, 64], P('lon'), may hold values from 2 to 3
- key_gain: float32 [16, 64], P('lon'), may hold values from 2 to 3
- w_gate_up: bfloat16 [2, 4096, 1024], P(None, 'lon'), may hold values from -0.1875 to 0.1875
- w_out: bfloat16 [1024, 1024], P('lon'), may hold values from -0.1875 to 0.1875
- w_down: bfloat16 [4096, 1024], P('lon'), may hold values from -0.09375 to 0.09375
Outputs:
- processed: bfloat16 [4, 8192, 1024], P('section', ('lat', 'lon'))
The draws below stay inside these ranges and needn't reach their ends.
All inputs are finite; a program needn't handle non-finite values.
Results may differ from the reference program's by a relative error of at most 0.02.
Values may be sent and summed in bfloat16 or wider, within the bound.
No kernel may reach another device: no remote copies, remote signals or barrier semaphores. Data moves between devices by JAX's collectives and lax.ppermute only.
A program may use at most 128 MiB of HBM per device.

```python
import jax
import jax.numpy as jnp
from jax import lax

V = 69
D = 1024
FF = 4096
HEADS = 16
HD = 64
NMEM = 50
PATCH = 8
KS = 10
ENS = 4
H = 512
W = 1024
PROWS = 64
PCOLS = 128
TOKENS = 8192
HEADS_LON = 1
FF_LON = 256
N_LON = 16


def place_ends(drawn, key, low, high):
    shape = drawn.shape
    spot = [jax.random.randint(jax.random.fold_in(key, axis), (), 0, shape[axis]) for axis in range(len(shape))]
    drawn = drawn.at[tuple(spot)].set(low)
    longest = shape.index(max(shape))
    spot[longest] = (spot[longest] + 1) % shape[longest]
    return drawn.at[tuple(spot)].set(high)


def block_levels(key, dims, shards, least, high):
    level = 1.0
    for dim, shards_of in shards:
        draws = jax.random.uniform(jax.random.fold_in(jax.random.fold_in(key, 6), dim), (shards_of,), jnp.float32, least / len(shards), high / len(shards))
        level = level * jnp.repeat(jnp.exp(draws), dims[dim] // shards_of).reshape((-1,) + (1,) * (len(dims) - 1 - dim))
    return level


def normal_values(key, dims, deviation, reach, pieces=(), kind=jnp.bfloat16):
    entries = deviation * jax.random.normal(key, dims, jnp.float32)
    if pieces:
        entries = entries * block_levels(key, dims, pieces, -0.22, 0.18)
    return jnp.clip(entries, -reach, reach).astype(kind)


def setup_inputs(seed: int = 0) -> dict:
    keys = jax.random.split(jax.random.key(seed), 14)
    fields = normal_values(keys[0], (ENS, V, H, W), 1.0, 6.0, ((2, 8), (3, 16)))
    embed_weight = normal_values(keys[1], (KS, KS, V, D), (KS * KS * V) ** -0.5, 0.078125, ((0, 2),))
    embed_bias = normal_values(keys[2], (D,), 0.5, 3.0)
    pos_embed = normal_values(keys[3], (PROWS, PCOLS, D), 1.0, 6.0, ((0, 8), (1, 16)))
    member_ids = place_ends(jax.random.randint(keys[4], (ENS,), 0, NMEM), jax.random.fold_in(keys[4], 1), 0, NMEM - 1).astype(jnp.int32)
    member_table = normal_values(keys[5], (NMEM, D), 1.0, 6.0)
    norm_gain = jnp.clip(1.0 + 0.1 * jax.random.normal(keys[6], (D,), jnp.float32), 0.5, 1.5)
    w_qkv = normal_values(keys[7], (3, HEADS * HD, D), D ** -0.5, 0.1875, ((1, 16),))
    query_gain = jnp.clip(2.0 + 1.0 * jax.random.uniform(keys[8], (HEADS, HD), jnp.float32) ** block_levels(keys[8], (HEADS, HD), ((0, 16),), -0.2, 0.2), 2.0, 3.0)
    key_gain = jnp.clip(2.0 + 1.0 * jax.random.uniform(keys[9], (HEADS, HD), jnp.float32) ** block_levels(keys[9], (HEADS, HD), ((0, 16),), -0.2, 0.2), 2.0, 3.0)
    w_gate_up = normal_values(keys[10], (2, FF, D), D ** -0.5, 0.1875, ((1, 16),))
    w_out = normal_values(keys[11], (HEADS * HD, D), (HEADS * HD) ** -0.5, 0.1875, ((0, 16),))
    w_down = normal_values(keys[12], (FF, D), FF ** -0.5, 0.09375, ((0, 16),))
    return {"fields": fields, "embed_weight": embed_weight, "embed_bias": embed_bias, "pos_embed": pos_embed, "member_ids": member_ids, "member_table": member_table, "norm_gain": norm_gain, "w_qkv": w_qkv, "query_gain": query_gain, "key_gain": key_gain, "w_gate_up": w_gate_up, "w_out": w_out, "w_down": w_down}


layer_epsilon = 1e-05
head_epsilon = 1e-06

def embed_member(padded_member, embed_weight):
    running = jnp.zeros((PROWS * PCOLS, D), jnp.float32)
    for row_off in range(KS):
        strip = padded_member[:, row_off:row_off + PATCH * (PROWS - 1) + 1:PATCH, :]
        columns = jnp.stack([strip[:, :, col_off:col_off + PATCH * (PCOLS - 1) + 1:PATCH] for col_off in range(KS)], 0)
        features = columns.reshape(KS * V, PROWS * PCOLS)
        running = running + lax.dot_general(features, embed_weight[row_off].reshape(KS * V, D), (((0,), (0,)), ((), ())), preferred_element_type=jnp.float32)
    return running

def attend_head(packed):
    queries, keys_normed, values = packed
    scores = jnp.dot(queries, keys_normed.T, preferred_element_type=jnp.float32) * HD ** (-0.5)
    weights = jnp.exp(scores)
    denominator = lax.optimization_barrier(jnp.sum(weights, axis=1))
    numerator = jnp.dot(weights.astype(jnp.bfloat16), values, preferred_element_type=jnp.float32)
    return (numerator / denominator[:, None]).astype(jnp.bfloat16)

def head_norm(part, gain):
    scale = lax.rsqrt(lax.optimization_barrier(jnp.mean(part * part, axis=-1, keepdims=True)) + head_epsilon)
    return (part * scale * gain).astype(jnp.bfloat16)

def process_member(tokens, norm_gain, w_qkv, query_gain, key_gain, w_gate_up, w_out, w_down):
    residual = tokens.astype(jnp.float32)
    average = lax.optimization_barrier(jnp.mean(residual, axis=-1, keepdims=True))
    centered = residual - average
    variance = lax.optimization_barrier(jnp.mean(centered * centered, axis=-1, keepdims=True))
    normed = (centered * lax.rsqrt(variance + layer_epsilon) * norm_gain).astype(jnp.bfloat16)
    projected = lax.dot_general(normed, w_qkv.reshape(3 * HEADS * HD, D), (((1,), (1,)), ((), ())), preferred_element_type=jnp.float32)
    projected = projected.reshape(TOKENS, 3, HEADS, HD)
    queries = head_norm(projected[:, 0], query_gain)
    keys_normed = head_norm(projected[:, 1], key_gain)
    values = projected[:, 2].astype(jnp.bfloat16)
    attended = lax.map(attend_head, (jnp.transpose(queries, (1, 0, 2)), jnp.transpose(keys_normed, (1, 0, 2)), jnp.transpose(values, (1, 0, 2))))
    attended = jnp.transpose(attended, (1, 0, 2)).reshape(TOKENS, HEADS * HD)
    gate_up = lax.dot_general(normed, w_gate_up.reshape(2 * FF, D), (((1,), (1,)), ((), ())), preferred_element_type=jnp.float32)
    hidden = (jax.nn.silu(gate_up[:, :FF]) * gate_up[:, FF:]).astype(jnp.bfloat16)
    head_width = HEADS_LON * HD
    summed = jnp.zeros((TOKENS, D), jnp.float32)
    for group in range(N_LON):
        head_lo = group * head_width
        unit_lo = group * FF_LON
        partial_value = jnp.dot(attended[:, head_lo:head_lo + head_width], w_out[head_lo:head_lo + head_width], preferred_element_type=jnp.float32)
        partial_value = partial_value + jnp.dot(hidden[:, unit_lo:unit_lo + FF_LON], w_down[unit_lo:unit_lo + FF_LON], preferred_element_type=jnp.float32)
        rounded = lax.optimization_barrier(partial_value.astype(jnp.bfloat16))
        summed = summed + rounded.astype(jnp.float32)
    return (residual + summed).astype(jnp.bfloat16)

def reference(fields, embed_weight, embed_bias, pos_embed, member_ids, member_table, norm_gain, w_qkv, query_gain, key_gain, w_gate_up, w_out, w_down):
    padded = jnp.pad(fields, ((0, 0), (0, 0), (1, 1), (0, 0)))
    padded = jnp.concatenate([padded[:, :, :, -1:], padded, padded[:, :, :, :1]], axis=3)
    one_hot = (member_ids[:, None] == jnp.arange(NMEM, dtype=jnp.int32)[None, :]).astype(jnp.bfloat16)
    member_vecs = jnp.dot(one_hot, member_table, preferred_element_type=jnp.float32)
    positions = pos_embed.reshape(TOKENS, D).astype(jnp.float32)
    outputs = []
    for member in range(ENS):
        embedded = embed_member(padded[member], embed_weight)
        tokens = (embedded + embed_bias.astype(jnp.float32) + positions + member_vecs[member][None, :]).astype(jnp.bfloat16)
        outputs.append(process_member(tokens, norm_gain, w_qkv, query_gain, key_gain, w_gate_up, w_out, w_down))
    return jnp.stack(outputs, 0)
```

```python
import functools

import jax
import jax.numpy as jnp
from jax import lax
from jax.experimental import pallas as pl
from jax.experimental.pallas import tpu as pltpu
from jax.sharding import Mesh, PartitionSpec as P

PATCH = 8
layer_epsilon = 1e-05
head_epsilon = 1e-06
LOG2E = 1.4426950408889634
HEAD = 64

X, CORE, YH, Z, YL = 4, 2, 2, 8, 2
LAT = ("x", "core")
LON = ("yh", "z")
ROW_ORDER = (0, 4, 1, 5, 2, 6, 3, 7)


def swap(array, axis):
    return lax.ppermute(array, axis, [(0, 1), (1, 0)])


def other_half_weights(array):
    return lax.ppermute(array, ("yh", "yl"), [(0, 3), (3, 0), (1, 2), (2, 1)])


def halo(f, section):
    lats, lons = X * CORE, YH * Z
    rows = jnp.where(section == 0, f[:, -1:], f[:, :1])
    pairs = [(2 * i, 2 * i + 2) for i in range(lats - 1)]
    pairs += [(2 * i + 1, 2 * i - 1) for i in range(1, lats)]
    row = lax.ppermute(rows, LAT + ("yl",), pairs)
    ext = jnp.concatenate([row, f, row], 1)
    ext = lax.dynamic_slice_in_dim(ext, section * 5, 61, 1)
    low = lax.ppermute(ext[:, :, -1:], LON, [(i, (i + 1) % lons) for i in range(lons)])
    high = lax.ppermute(ext[:, :, :1], LON, [((i + 1) % lons, i) for i in range(lons)])
    return jnp.concatenate([low, ext, high], 2)


def attend_kernel(bk, q_ref, kv_ref, o_ref, v1):
    chunks, _, nk = kv_ref.shape
    bq = q_ref.shape[0]

    @pl.when(pl.program_id(0) == 0)
    def _():
        for c in range(chunks):
            for b in range(0, nk, 512):
                rows = kv_ref[c, HEAD:, b : b + 512]
                stacked = jnp.concatenate([rows, jnp.ones_like(rows)], 0)
                v1[pl.ds(c * nk + b, 512), :] = stacked.T

    q = q_ref[...]

    def body(c, acc):
        for b in range(0, nk, bk):
            scores = jnp.dot(q, kv_ref[c, :HEAD, b : b + bk], preferred_element_type=jnp.float32)
            weights = jnp.exp2(scores).astype(jnp.bfloat16)
            values = v1[pl.ds(pl.multiple_of(c * nk + b, bk), bk), :]
            acc = acc + jnp.dot(weights, values, preferred_element_type=jnp.float32)
        return acc

    acc = lax.fori_loop(0, chunks, body, jnp.zeros((bq, 2 * HEAD), jnp.float32))
    o_ref[...] = (acc / pltpu.roll(acc, HEAD, 1))[:, :HEAD].astype(jnp.bfloat16)


def attend(q, kv, bq=1024, bk=256):
    n = q.shape[0]
    keys = kv.shape[0] * kv.shape[2]
    return pl.pallas_call(
        functools.partial(attend_kernel, bk),
        grid=(n // bq,),
        in_specs=[
            pl.BlockSpec((bq, HEAD), lambda i: (i, 0)),
            pl.BlockSpec(kv.shape, lambda i: (0, 0, 0)),
        ],
        out_specs=pl.BlockSpec((bq, HEAD), lambda i: (i, 0)),
        out_shape=jax.ShapeDtypeStruct((n, HEAD), jnp.bfloat16),
        scratch_shapes=[pltpu.VMEM((keys, 2 * HEAD), jnp.bfloat16)],
        compiler_params=pltpu.CompilerParams(vmem_limit_bytes=40 * 2**20),
        cost_estimate=pl.CostEstimate(
            flops=4 * n * keys * HEAD, bytes_accessed=4 * 2**20, transcendentals=n * keys
        ),
    )(q, kv)


def shards(
    fields,
    embed_weight,
    embed_bias,
    pos_embed,
    member_ids,
    member_table,
    norm_gain,
    w_qkv,
    query_gain,
    key_gain,
    w_gate_up,
    w_out,
    w_down,
):
    f32, bf16 = jnp.float32, jnp.bfloat16
    width = embed_weight.shape[3]
    yl = lax.axis_index("yl")
    yh = lax.axis_index("yh")
    core = lax.axis_index("core")

    gains = jnp.concatenate([query_gain, key_gain], 0)
    gains_other = other_half_weights(gains)
    w_qkv_other = other_half_weights(w_qkv)
    w_gu_other = other_half_weights(w_gate_up)
    w_down_other = other_half_weights(w_down)
    w_out_all = lax.all_gather(w_out, LON, axis=0, tiled=True)

    f = jnp.transpose(fields, (0, 2, 3, 1))
    padded = halo(f, yl)
    part = lax.conv_general_dilated(
        padded,
        embed_weight,
        (PATCH, PATCH),
        "VALID",
        dimension_numbers=("NHWC", "HWIO", "NHWC"),
        preferred_element_type=f32,
    )
    keep = lax.dynamic_slice_in_dim(part, 2 * yl, 2, 0)
    send = lax.dynamic_slice_in_dim(part, 2 - 2 * yl, 2, 0)
    embedded = keep + swap(send.astype(bf16), "yl").astype(f32)
    one_hot = (
        member_ids[:, None] == jnp.arange(member_table.shape[0], dtype=jnp.int32)[None, :]
    ).astype(bf16)
    member_vecs = jnp.dot(one_hot, member_table, preferred_element_type=f32)
    tokens = (
        embedded
        + embed_bias.astype(f32)
        + pos_embed.astype(f32)[None]
        + member_vecs[:, None, None, :]
    ).astype(bf16)
    residual = tokens.astype(f32)
    average = jnp.mean(residual, axis=-1, keepdims=True)
    centered = residual - average
    variance = jnp.mean(centered * centered, axis=-1, keepdims=True)
    normed = (centered * lax.rsqrt(variance + layer_epsilon) * norm_gain).astype(bf16)

    def row_major(a):
        return jnp.stack([a[:, r] for r in ROW_ORDER], 0)

    normed_all = lax.all_gather(row_major(normed), "z", axis=2, tiled=True)
    n_tok = normed_all.shape[0] * normed_all.shape[1] * normed_all.shape[2]
    flat = normed_all.reshape(n_tok, width)

    w_both = jnp.stack([w_qkv, w_qkv_other], 0).reshape(6 * HEAD, width)
    projected = lax.dot_general(w_both, flat, (((1,), (1,)), ((), ())), preferred_element_type=f32)
    projected = projected.reshape(2, 3, HEAD, 8, 2, 64)
    gain_both = jnp.stack([gains, gains_other], 0)

    def head_norm(part, gain):
        scale = lax.rsqrt(jnp.mean(part * part, axis=1, keepdims=True) + head_epsilon)
        return part * scale * gain[:, :, None, None, None]

    queries = (head_norm(projected[:, 0], gain_both[:, 0]) * (LOG2E / 8.0)).astype(bf16)
    keys = head_norm(projected[:, 1], gain_both[:, 1]).astype(bf16)
    values = projected[:, 2].astype(bf16)
    qkv = jnp.concatenate([queries, keys, values], 1)
    mine = lax.dynamic_index_in_dim(qkv, core, 3, keepdims=False)
    theirs = lax.dynamic_index_in_dim(qkv, 1 - core, 3, keepdims=False)
    mine = mine.reshape(2, 3 * HEAD, 512)
    theirs = theirs.reshape(2, 3 * HEAD, 512)
    both_axes = ("core", "yh")
    got_yh = lax.ppermute(mine[1], both_axes, [(0, 1), (1, 0), (2, 3), (3, 2)])
    got_core = lax.ppermute(theirs[0], both_axes, [(0, 2), (2, 0), (1, 3), (3, 1)])
    got_both = lax.ppermute(theirs[1], both_axes, [(0, 3), (3, 0), (1, 2), (2, 1)])
    blocks = jnp.stack([mine[0], got_yh, got_core, got_both], 0)
    kv_own = jnp.transpose(blocks[:, HEAD:], (1, 0, 2)).reshape(2 * HEAD, 2048)
    kv = lax.all_gather(kv_own, "x", axis=0, tiled=False)

    q = blocks[:, :HEAD].reshape(2, 2, HEAD, 8, 64)
    q = jnp.where(yh == 0, q, q[:, ::-1])
    q = jnp.where(core == 0, q, q[::-1])
    q = jnp.stack([q[:, :, :, ROW_ORDER.index(r)] for r in range(8)], 1)
    q = jnp.transpose(q, (0, 1, 2, 4, 3)).reshape(2048, HEAD)

    units = w_down.shape[0]
    w_gu = jnp.stack([w_gate_up, w_gu_other], 1).reshape(4 * units, width)
    gate_up = lax.dot_general(flat, w_gu, (((1,), (1,)), ((), ())), preferred_element_type=f32)
    hidden = (jax.nn.silu(gate_up[:, : 2 * units]) * gate_up[:, 2 * units :]).astype(bf16)
    update = jnp.dot(hidden, jnp.concatenate([w_down, w_down_other], 0), preferred_element_type=f32)
    update = update.reshape(8, 2, Z, 8, width)
    own_here = (jnp.arange(Z) == lax.axis_index("z"))[None, None, :, None, None]
    update = update + jnp.where(own_here, row_major(tokens)[:, :, None].astype(f32), 0.0)
    update = update.astype(bf16).reshape(8, 2, Z * 8, width)
    summed = lax.psum_scatter(update, "z", scatter_dimension=0, tiled=True)[0]
    final_pairs = []
    for s in range(YH):
        for z in range(Z):
            row = ROW_ORDER[z]
            final_pairs.append((s * Z + z, 2 * row + s))
    summed = lax.ppermute(summed, LON, final_pairs)

    attended = attend(q, kv)
    attended = lax.all_to_all(
        attended.reshape(CORE * YH * Z, 64, HEAD), ("core", "yh", "z"), 0, 0, tiled=True
    )
    attended = attended.reshape(CORE, YH * Z, 64, HEAD)
    attended = jnp.transpose(attended, (0, 2, 1, 3)).reshape(CORE * 64, YH * Z * HEAD)
    mixed = jnp.dot(attended, w_out_all, preferred_element_type=f32).reshape(2, 64, width)
    return (summed.astype(f32) + mixed).astype(bf16)


def solution(mesh):
    chips = Mesh(mesh.devices.reshape(X, CORE, YH, Z, YL), ("x", "core", "yh", "z", "yl"))
    return jax.shard_map(
        shards,
        mesh=chips,
        in_specs=(
            P(None, None, LAT, LON),
            P("yl", None, None, None),
            P(),
            P(LAT, LON, None),
            P("yl"),
            P(),
            P(),
            P(None, LON, None),
            P(LON, None),
            P(LON, None),
            P(None, LON, None),
            P(LON, None),
            P(LON, None),
        ),
        out_specs=P("yl", LAT + LON, None),
        check_vma=False,
    )
```

```python
import functools

import jax
import jax.numpy as jnp
from jax import lax
from jax.experimental import pallas as pl
from jax.experimental.pallas import tpu as pltpu
from jax.sharding import Mesh, PartitionSpec as P

PATCH = 8
layer_epsilon = 1e-05
head_epsilon = 1e-06
LOG2E = 1.4426950408889634
HEAD = 64

X, CORE, YH, Z, YL = 4, 2, 2, 8, 2
LAT = ("x", "core")
LON = ("yh", "z")


def other_half_weights(array):
    return lax.ppermute(array, ("yh", "yl"), [(0, 3), (3, 0), (1, 2), (2, 1)])


def edges_kernel(s_ref, top_ref, left_ref, right_ref, row_ref, low_ref, high_ref, wide):
    row_ref[...] = top_ref[:, 0]
    members, rows, cols, channels = right_ref.shape
    wide[..., :channels] = right_ref[...].reshape(wide.shape[0], cols, channels).astype(jnp.float32)
    low = wide[:, cols - 1, :channels]
    low_ref[...] = low.reshape(low_ref.shape).astype(jnp.bfloat16)
    wide[..., :channels] = left_ref[...].reshape(wide.shape[0], cols, channels).astype(jnp.float32)
    high = wide[:, 0, :channels]
    high_ref[...] = high.reshape(high_ref.shape).astype(jnp.bfloat16)


def edges(f, ids):
    members, rows, cols, channels = f.shape
    column = (members, rows, 16, channels)
    line = jax.ShapeDtypeStruct((members, rows, channels), f.dtype)
    whole = pl.BlockSpec((members, rows, channels), lambda i, s: (0, 0, 0))
    return pl.pallas_call(
        edges_kernel,
        grid_spec=pltpu.PrefetchScalarGridSpec(
            num_scalar_prefetch=1,
            grid=(1,),
            in_specs=[
                pl.BlockSpec(
                    (members, 1, cols, channels), lambda i, s: (0, (1 - s[0]) * (rows - 1), 0, 0)
                ),
                pl.BlockSpec(column, lambda i, s: (0, 0, 0, 0)),
                pl.BlockSpec(column, lambda i, s: (0, 0, cols // 16 - 1, 0)),
            ],
            out_specs=[whole] * 3,
            scratch_shapes=[pltpu.VMEM((members * rows, 16, 128), jnp.float32)],
        ),
        out_shape=[line] * 3,
        compiler_params=pltpu.CompilerParams(vmem_limit_bytes=40 * 2**20),
    )(ids, f, f, f)


def halo(f, ids, section):
    lats, lons = X * CORE, YH * Z
    row, low, high = edges(f, ids)
    to_lat = [(2 * i, 2 * i + 2) for i in range(lats - 1)]
    to_lat += [(2 * i + 1, 2 * i - 1) for i in range(1, lats)]
    forward = [(i, (i + 1) % lons) for i in range(lons)]
    backward = [(target, source) for source, target in forward]
    row = lax.ppermute(row, LAT + ("yl",), to_lat)

    def column(edge, corner, pairs):
        edge = jnp.concatenate([edge, corner[:, None]], 1)
        edge = lax.ppermute(edge, LON, pairs)
        edge = jnp.concatenate([edge[:, -1:], edge, jnp.zeros_like(edge[:, :3])], 1)
        edge = lax.dynamic_slice_in_dim(edge, section * 5, 64, 1)
        edge = edge.reshape(2, 2, 2, 4, 8, edge.shape[-1])[:, :, :, :, :5].astype(jnp.float32)
        return jnp.transpose(edge, (4, 2, 0, 3, 1, 5)).reshape(5, 32, edge.shape[-1])

    return row, column(low, row[:, -1], forward), column(high, row[:, 0], backward)


def embed_kernel(
    ids_ref, f_ref, row_ref, low_ref, high_ref, w_ref, pos_ref, out_ref, xf, rhs, acc
):
    step = pl.program_id(0)
    section = ids_ref[0]
    channels = f_ref.shape[4]
    offset = step - 1 + 5 * section
    shift = jnp.where(offset < 0, -1, jnp.where(offset > 7, 1, 0))

    @pl.when(step == 0)
    def _():
        xf[...] = jnp.zeros_like(xf)
        rhs[...] = jnp.zeros_like(rhs)
        acc[...] = jnp.zeros_like(acc)

    for slot in range(32):
        patch = slot // 16 * 4 + slot // 2 % 4
        member = slot // 8 % 2 * 2 + slot % 2
        at = patch + shift
        value = f_ref[member, jnp.clip(at, 0, 7), 0]
        if patch in (0, 7):
            value = jnp.where((at < 0) | (at > 7), row_ref[member], value)
        xf[slot, 8:72, :channels] = value.astype(jnp.float32)
        xf[slot, 7:8, :channels] = low_ref[0, slot : slot + 1]
        xf[slot, 72:73, :channels] = high_ref[0, slot : slot + 1]
    taps = w_ref.shape[1]
    columns = []
    for b in range(taps):
        rhs[b * 128 : b * 128 + channels, :] = w_ref[0, b]
        column = xf[:, pl.ds(7 + b, 8, stride=8), :]
        columns.append(column.reshape(256, 128).astype(jnp.bfloat16))
    lhs = jnp.concatenate(columns, 1)
    acc[...] += jnp.dot(lhs, rhs[...], preferred_element_type=jnp.float32)

    @pl.when(step == pl.num_programs(0) - 1)
    def _():
        first = jnp.where(section == 0, 1.0, 0.0)
        for slot in range(32):
            patch = slot // 16 * 4 + slot // 2 % 4
            rows = slice(8 * slot, 8 * slot + 8)
            acc[rows, :] += first * pos_ref[patch].astype(jnp.float32)
        out_ref[...] = acc[...].astype(jnp.bfloat16)


def embed(f, row, low, high, weight, pos, ids):
    taps, cols, channels, width = weight.shape
    members, rows, wide, _ = f.shape
    whole = lambda n: (lambda i, s: (0,) * n)
    return pl.pallas_call(
        embed_kernel,
        grid_spec=pltpu.PrefetchScalarGridSpec(
            num_scalar_prefetch=1,
            grid=(taps,),
            in_specs=[
                pl.BlockSpec(
                    (members, 8, 1, wide, channels),
                    lambda i, s: (0, 0, (i + 7 + 5 * s[0]) % 8, 0, 0),
                ),
                pl.BlockSpec(row.shape, whole(3)),
                pl.BlockSpec((1, 32, channels), lambda i, s: (i, 0, 0)),
                pl.BlockSpec((1, 32, channels), lambda i, s: (i, 0, 0)),
                pl.BlockSpec((1, cols, channels, width), lambda i, s: (i, 0, 0, 0)),
                pl.BlockSpec(pos.shape, whole(3)),
            ],
            out_specs=pl.BlockSpec((256, width), whole(2)),
            scratch_shapes=[
                pltpu.VMEM((32, 80, 128), jnp.float32),
                pltpu.VMEM((cols * 128, width), jnp.bfloat16),
                pltpu.VMEM((256, width), jnp.float32),
            ],
        ),
        out_shape=jax.ShapeDtypeStruct((256, width), jnp.bfloat16),
        compiler_params=pltpu.CompilerParams(vmem_limit_bytes=52 * 2**20),
        cost_estimate=pl.CostEstimate(
            flops=8 * 10**9, bytes_accessed=12 * 2**20, transcendentals=0
        ),
    )(ids, f.reshape(members, 8, rows // 8, wide, channels), row, low, high, weight, pos)


def attend_kernel(last, ids_ref, q_ref, kv_ref, *refs):
    acc_refs, o_ref, v1 = refs[:-2], refs[-2], refs[-1]
    blocks, _, nk = kv_ref.shape
    bq = q_ref.shape[0]
    bk = 256

    @pl.when(pl.program_id(0) == 0)
    def _():
        for c in range(blocks):
            rows = kv_ref[c, HEAD:, :]
            stacked = jnp.concatenate([rows, jnp.ones_like(rows)], 0)
            v1[pl.ds(c * nk, nk), :] = stacked.T

    q = q_ref[...]

    def body(c, acc):
        for b in range(0, nk, bk):
            scores = jnp.dot(q, kv_ref[c, :HEAD, b : b + bk], preferred_element_type=jnp.float32)
            weights = jnp.exp2(scores).astype(jnp.bfloat16)
            values = v1[pl.ds(pl.multiple_of(c * nk + b, bk), bk), :]
            acc = acc + jnp.dot(weights, values, preferred_element_type=jnp.float32)
        return acc

    if acc_refs:
        acc = acc_refs[0][...]
    else:
        acc = jnp.zeros((bq, 2 * HEAD), jnp.float32)
    acc = lax.fori_loop(0, blocks, body, acc, unroll=2)
    if last:
        halves = (acc / pltpu.roll(acc, HEAD, 1)).reshape(bq // 64, 2, 32, 2 * HEAD)
        left, right = halves[:, 0], halves[:, 1]
        right = pltpu.roll(right.reshape(bq // 2, 2 * HEAD), HEAD, 1).reshape(left.shape)
        lane = lax.broadcasted_iota(jnp.int32, left.shape, 2)
        packed = jnp.where(lane < HEAD, left, right).astype(jnp.bfloat16)
        half = packed.shape[0] // 2
        yh = ids_ref[3]
        o_ref[pl.ds(yh * half, half)] = packed[:half]
        o_ref[pl.ds(half - yh * half, half)] = packed[half:]
    else:
        o_ref[...] = acc


def attend(ids, q, kv, acc=None, last=False):
    n = q.shape[0]
    bq = n // CORE
    keys = kv.shape[0] * kv.shape[2]
    rows = lambda w: pl.BlockSpec((bq, w), lambda i, s: (i, 0))
    if last:
        out_spec = pl.BlockSpec((bq // 64, 32, 2 * HEAD), lambda i, s: ((i + s[1]) % CORE, 0, 0))
        out_shape = jax.ShapeDtypeStruct((n // 64, 32, 2 * HEAD), jnp.bfloat16)
    else:
        out_spec = rows(2 * HEAD)
        out_shape = jax.ShapeDtypeStruct((n, 2 * HEAD), jnp.float32)
    return pl.pallas_call(
        functools.partial(attend_kernel, last),
        grid_spec=pltpu.PrefetchScalarGridSpec(
            num_scalar_prefetch=1,
            grid=(CORE,),
            in_specs=[rows(HEAD), pl.BlockSpec(kv.shape, lambda i, s: (0, 0, 0))]
            + ([rows(2 * HEAD)] if acc is not None else []),
            out_specs=out_spec,
            scratch_shapes=[pltpu.VMEM((keys, 2 * HEAD), jnp.bfloat16)],
        ),
        out_shape=out_shape,
        compiler_params=pltpu.CompilerParams(vmem_limit_bytes=40 * 2**20),
        cost_estimate=pl.CostEstimate(
            flops=64 * n * keys * HEAD, bytes_accessed=4 * 2**20, transcendentals=n * keys
        ),
    )(ids, q, kv, *([acc] if acc is not None else []))


def ring_z(own, beside, parts=1):
    z = lax.axis_index("z")
    rows, members, cols, width = own.shape
    size = rows // parts
    forward = [(i, (i + 1) % Z) for i in range(Z)]
    backward = [(target, source) for source, target in forward]
    out = jnp.zeros((rows, members, Z * cols, width), own.dtype)

    def place(out, shard, part, at):
        return lax.dynamic_update_slice(out, shard, (part * size, 0, (at % Z) * cols, 0))

    out = place(out, own, 0, z)
    ups = [own[p * size : (p + 1) * size] for p in range(parts)]
    downs = list(ups)
    for step in range(1, Z // 2 + 1):
        for p in range(parts):
            ups[p] = lax.ppermute(ups[p], "z", forward)
            if step < Z // 2:
                downs[p] = lax.ppermute(downs[p], "z", backward)
        if step == 2:
            ups, downs, beside = lax.optimization_barrier((ups, downs, beside))
        for p in range(parts):
            out = place(out, ups[p], p, z - step + Z)
            if step < Z // 2:
                out = place(out, downs[p], p, z + step)
    return out, beside


def project_kernel(ids_ref, x_ref, own_ref, other_ref, gain_ref, *out_refs):
    core = ids_ref[1]
    for rel_core in range(2):
        member = core if rel_core == 0 else 1 - core
        x = x_ref[:, member].reshape(-1, x_ref.shape[3])
        for rel_head, w in enumerate((own_ref[...], other_ref[: 3 * HEAD])):
            out = lax.dot_general(
                w, x, (((1,), (1,)), ((), ())), preferred_element_type=jnp.float32
            )
            out_ref = out_refs[2 * rel_core + rel_head]
            for kind in range(2):
                part = out[kind * HEAD : (kind + 1) * HEAD]
                mean = jnp.mean(part * part, axis=0, keepdims=True)
                part = part * lax.rsqrt(mean + head_epsilon) * gain_ref[rel_head, kind]
                if kind == 0:
                    part = part * (LOG2E / 8.0)
                out_ref[kind * HEAD : (kind + 1) * HEAD, :] = part.astype(jnp.bfloat16)
            out_ref[2 * HEAD :, :] = out[2 * HEAD :].astype(jnp.bfloat16)


def project(x, own, other, gains, ids):
    tokens = x.shape[0] * x.shape[2]
    whole = lambda a: pl.BlockSpec(a.shape, lambda i, s: (0,) * a.ndim)
    out = jax.ShapeDtypeStruct((3 * HEAD, tokens), jnp.bfloat16)
    return pl.pallas_call(
        project_kernel,
        grid_spec=pltpu.PrefetchScalarGridSpec(
            num_scalar_prefetch=1,
            grid=(1,),
            in_specs=[whole(x), whole(own), whole(other), whole(gains)],
            out_specs=[whole(out)] * 4,
        ),
        out_shape=[out] * 4,
        compiler_params=pltpu.CompilerParams(vmem_limit_bytes=32 * 2**20),
        cost_estimate=pl.CostEstimate(flops=3 * 10**9, bytes_accessed=4 * 2**20, transcendentals=0),
    )(ids, x, own, other, gains)


def mlp_kernel(ids_ref, x_ref, tok_ref, gu_ref, down_ref, other_ref, o_ref, acc):
    rows, members, cols, width = x_ref.shape
    units = down_ref.shape[0]
    x = x_ref[...].reshape(-1, width)
    contract = (((1,), (1,)), ((), ()))
    other = [other_ref[n * units : (n + 1) * units] for n in range(3)]
    total = None
    for gate_w, up_w, down_w in ((gu_ref[0], gu_ref[1], down_ref[...]), other):
        gate = lax.dot_general(x, gate_w, contract, preferred_element_type=jnp.float32)
        up = lax.dot_general(x, up_w, contract, preferred_element_type=jnp.float32)
        hidden = (gate / (1.0 + jnp.exp(-gate)) * up).astype(jnp.bfloat16)
        term = jnp.dot(hidden, down_w, preferred_element_type=jnp.float32)
        total = term if total is None else total + term
    acc[...] = total.reshape(acc.shape)
    at = pl.multiple_of(ids_ref[2] * 8, 8)
    acc[:, :, pl.ds(at, 8), :] += tok_ref[...].astype(jnp.float32)
    o_ref[...] = acc[...].astype(jnp.bfloat16)


def mlp(x, tokens, gu, down, other, ids, rows=4):
    whole = lambda a: pl.BlockSpec(a.shape, lambda i, s: (0,) * a.ndim)
    block = lambda a: pl.BlockSpec((rows,) + a.shape[1:], lambda i, s: (i, 0, 0, 0))
    return pl.pallas_call(
        mlp_kernel,
        grid_spec=pltpu.PrefetchScalarGridSpec(
            num_scalar_prefetch=1,
            grid=(x.shape[0] // rows,),
            in_specs=[block(x), block(tokens)] + [whole(a) for a in (gu, down, other)],
            out_specs=block(x),
            scratch_shapes=[pltpu.VMEM((rows,) + x.shape[1:], jnp.float32)],
        ),
        out_shape=jax.ShapeDtypeStruct(x.shape, jnp.bfloat16),
        compiler_params=pltpu.CompilerParams(vmem_limit_bytes=32 * 2**20),
        cost_estimate=pl.CostEstimate(flops=6 * 10**9, bytes_accessed=8 * 2**20, transcendentals=0),
    )(ids, x, tokens, gu, down, other)


def shards(
    fields,
    embed_weight,
    embed_bias,
    pos_embed,
    member_ids,
    member_table,
    norm_gain,
    w_qkv,
    query_gain,
    key_gain,
    w_gate_up,
    w_out,
    w_down,
):
    f32, bf16 = jnp.float32, jnp.bfloat16
    width = embed_weight.shape[3]
    yl = lax.axis_index("yl")
    yh = lax.axis_index("yh")
    core = lax.axis_index("core")

    gains = jnp.concatenate([query_gain, key_gain], 0)
    coarse = lax.reduce_precision(gains, 8, 7)
    middle = lax.reduce_precision(gains - coarse, 8, 7)
    fine = gains - coarse - middle
    terms = jnp.stack([coarse, middle, fine], 0).astype(bf16).reshape(1, 6 * HEAD)
    terms = jnp.pad(terms, ((0, 15), (0, width - 6 * HEAD)))
    qkv_other = other_half_weights(jnp.concatenate([w_qkv.reshape(-1, width), terms], 0))
    mlp_other = other_half_weights(
        jnp.concatenate([w_gate_up.reshape(-1, width), w_down], 0)
    )
    terms = qkv_other[-16:, : 6 * HEAD][0].astype(f32).reshape(3, 2, HEAD)
    gains_other = terms[0] + terms[1] + terms[2]
    gain_both = jnp.stack([gains, gains_other], 0)[..., None]
    w_out_half = lax.all_gather(w_out, "z", axis=0, tiled=True)
    ids = jnp.stack([yl, core, lax.axis_index("z"), yh]).astype(jnp.int32)

    f = jnp.transpose(fields, (0, 2, 3, 1))
    row, low, high = halo(f, ids, yl)
    part = embed(f, row, low, high, embed_weight, pos_embed, ids)
    part = lax.all_to_all(part, ("yh", "yl"), 0, 0, tiled=True)
    part = part.reshape(YH, YL, 4, 2, 8, width).astype(f32)
    embedded = jnp.transpose(part[:, 0] + part[:, 1], (1, 0, 2, 3, 4)).reshape(8, 2, 8, width)
    one_hot = (
        member_ids[:, None] == jnp.arange(member_table.shape[0], dtype=jnp.int32)[None, :]
    ).astype(bf16)
    member_vecs = jnp.dot(one_hot, member_table, preferred_element_type=f32)
    tokens = (
        embedded
        + embed_bias.astype(f32)
        + member_vecs[None, :, None, :]
    ).astype(bf16)
    residual = tokens.astype(f32)
    average = jnp.mean(residual, axis=-1, keepdims=True)
    centered = residual - average
    variance = jnp.mean(centered * centered, axis=-1, keepdims=True)
    normed = (centered * lax.rsqrt(variance + layer_epsilon) * norm_gain).astype(bf16)

    normed_all, (w_out_half, qkv_other) = ring_z(normed, (w_out_half, qkv_other))

    normed_all, mlp_other = lax.optimization_barrier((normed_all, mlp_other))

    mine, mine_yh, theirs, theirs_yh = project(
        normed_all, w_qkv.reshape(3 * HEAD, width), qkv_other, gain_both, ids
    )
    pair = ("core", "yh")
    got_core = lax.ppermute(theirs, pair, [(0, 2), (2, 0), (1, 3), (3, 1)])
    got_yh = lax.ppermute(mine_yh, pair, [(0, 1), (1, 0), (2, 3), (3, 2)])
    got_both = lax.ppermute(theirs_yh, pair, [(0, 3), (3, 0), (1, 2), (2, 1)])
    got_core, normed_all = lax.optimization_barrier((got_core, normed_all))
    blocks = jnp.stack([mine, got_yh, got_core, got_both], 0)
    kv_own = blocks[:, HEAD:]

    x_up = [(i, (i + 1) % X) for i in range(X)]
    x_down = [(target, source) for source, target in x_up]
    first, second = kv_own[:2], kv_own[2:]
    near = [lax.ppermute(first, "x", x_up), lax.ppermute(second, "x", x_down)]
    late = [lax.ppermute(second, "x", x_up), lax.ppermute(first, "x", x_down)]
    far = [lax.ppermute(near[0], "x", x_up), lax.ppermute(near[1], "x", x_down)]

    q = jnp.transpose(blocks[:, :HEAD], (0, 2, 1)).reshape(-1, HEAD)

    update = mlp(normed_all, tokens, w_gate_up, w_down, mlp_other, ids)
    summed = lax.psum_scatter(update, "z", scatter_dimension=0, tiled=True)[0]

    acc = attend(ids, q, kv_own)
    acc, w_out_half = lax.optimization_barrier((acc, w_out_half))
    w_out_other = other_half_weights(w_out_half)
    acc = attend(ids, q, jnp.concatenate(near, 0), acc)
    acc = attend(ids, q, jnp.concatenate(late, 0), acc)
    attended = attend(ids, q, jnp.concatenate(far, 0), acc, last=True)
    attended = lax.all_to_all(attended, ("core", "yh", "z"), 0, 0, tiled=True)
    attended = attended.reshape(CORE, YH, Z, 32, 2, HEAD)
    attended = jnp.transpose(attended, (0, 4, 3, 1, 2, 5)).reshape(CORE * 64, YH * Z * HEAD)
    half = Z * HEAD
    own_cols = lax.dynamic_slice_in_dim(attended, yh * half, half, 1)
    other_cols = lax.dynamic_slice_in_dim(attended, half - yh * half, half, 1)
    mixed = jnp.dot(own_cols, w_out_half, preferred_element_type=f32)
    mixed = mixed + jnp.dot(other_cols, w_out_other, preferred_element_type=f32)
    mixed = mixed.reshape(2, 64, width)
    return (summed.astype(f32) + mixed).astype(bf16)


def solution(mesh):
    chips = Mesh(mesh.devices.reshape(X, CORE, YH, Z, YL), ("x", "core", "yh", "z", "yl"))
    return jax.shard_map(
        shards,
        mesh=chips,
        in_specs=(
            P(None, None, LAT, LON),
            P("yl", None, None, None),
            P(),
            P(LAT, LON, None),
            P("yl"),
            P(),
            P(),
            P(None, LON, None),
            P(LON, None),
            P(LON, None),
            P(None, LON, None),
            P(LON, None),
            P(LON, None),
        ),
        out_specs=P("yl", LAT + LON, None),
        check_vma=False,
    )
```

```python
import functools

import jax
import jax.numpy as jnp
from jax import lax
from jax.experimental import pallas as pl
from jax.experimental.pallas import tpu as pltpu
from jax.sharding import Mesh, PartitionSpec as P

PATCH = 8
layer_epsilon = 1e-05
head_epsilon = 1e-06
LOG2E = 1.4426950408889634
HEAD = 64

X, CORE, YH, Z, YL = 4, 2, 2, 8, 2
LAT = ("x", "core")
LON = ("yh", "z")


def other_half_weights(array):
    return lax.ppermute(array, ("yh", "yl"), [(0, 3), (3, 0), (1, 2), (2, 1)])


def edges_kernel(s_ref, top_ref, left_ref, right_ref, row_ref, low_ref, high_ref, wide):
    row_ref[...] = top_ref[:, 0]
    members, rows, cols, channels = right_ref.shape
    wide[..., :channels] = right_ref[...].reshape(wide.shape[0], cols, channels).astype(jnp.float32)
    low = wide[:, cols - 1, :channels]
    low_ref[...] = low.reshape(low_ref.shape).astype(jnp.bfloat16)
    wide[..., :channels] = left_ref[...].reshape(wide.shape[0], cols, channels).astype(jnp.float32)
    high = wide[:, 0, :channels]
    high_ref[...] = high.reshape(high_ref.shape).astype(jnp.bfloat16)


def edges(f, ids):
    members, rows, cols, channels = f.shape
    column = (members, rows, 16, channels)
    line = jax.ShapeDtypeStruct((members, rows, channels), f.dtype)
    whole = pl.BlockSpec((members, rows, channels), lambda i, s: (0, 0, 0))
    return pl.pallas_call(
        edges_kernel,
        grid_spec=pltpu.PrefetchScalarGridSpec(
            num_scalar_prefetch=1,
            grid=(1,),
            in_specs=[
                pl.BlockSpec(
                    (members, 1, cols, channels), lambda i, s: (0, (1 - s[0]) * (rows - 1), 0, 0)
                ),
                pl.BlockSpec(column, lambda i, s: (0, 0, 0, 0)),
                pl.BlockSpec(column, lambda i, s: (0, 0, cols // 16 - 1, 0)),
            ],
            out_specs=[whole] * 3,
            scratch_shapes=[pltpu.VMEM((members * rows, 16, 128), jnp.float32)],
        ),
        out_shape=[line] * 3,
        compiler_params=pltpu.CompilerParams(vmem_limit_bytes=40 * 2**20),
    )(ids, f, f, f)


def halo(f, ids, section):
    lats, lons = X * CORE, YH * Z
    row, low, high = edges(f, ids)
    to_lat = [(2 * i, 2 * i + 2) for i in range(lats - 1)]
    to_lat += [(2 * i + 1, 2 * i - 1) for i in range(1, lats)]
    forward = [(i, (i + 1) % lons) for i in range(lons)]
    backward = [(target, source) for source, target in forward]
    row = lax.ppermute(row, LAT + ("yl",), to_lat)

    def column(edge, corner, pairs):
        edge = jnp.concatenate([edge, corner[:, None]], 1)
        edge = lax.ppermute(edge, LON, pairs)
        edge = jnp.concatenate([edge[:, -1:], edge, jnp.zeros_like(edge[:, :3])], 1)
        edge = lax.dynamic_slice_in_dim(edge, section * 5, 64, 1)
        edge = edge.reshape(2, 2, 2, 4, 8, edge.shape[-1])[:, :, :, :, :5].astype(jnp.float32)
        return jnp.transpose(edge, (4, 2, 0, 3, 1, 5)).reshape(5, 32, edge.shape[-1])

    return row, column(low, row[:, -1], forward), column(high, row[:, 0], backward)


def embed_kernel(
    ids_ref, f_ref, row_ref, low_ref, high_ref, w_ref, pos_ref, out_ref, xf, rhs, acc
):
    step = pl.program_id(0)
    section = ids_ref[0]
    channels = f_ref.shape[4]
    offset = step - 1 + 5 * section
    shift = jnp.where(offset < 0, -1, jnp.where(offset > 7, 1, 0))

    @pl.when(step == 0)
    def _():
        xf[...] = jnp.zeros_like(xf)
        rhs[...] = jnp.zeros_like(rhs)
        acc[...] = jnp.zeros_like(acc)

    for slot in range(32):
        patch = slot // 16 * 4 + slot // 2 % 4
        member = slot // 8 % 2 * 2 + slot % 2
        at = patch + shift
        value = f_ref[member, jnp.clip(at, 0, 7), 0]
        if patch in (0, 7):
            value = jnp.where((at < 0) | (at > 7), row_ref[member], value)
        xf[slot, 8:72, :channels] = value.astype(jnp.float32)
        xf[slot, 7:8, :channels] = low_ref[0, slot : slot + 1]
        xf[slot, 72:73, :channels] = high_ref[0, slot : slot + 1]
    taps = w_ref.shape[1]
    columns = []
    for b in range(taps):
        rhs[b * 128 : b * 128 + channels, :] = w_ref[0, b]
        column = xf[:, pl.ds(7 + b, 8, stride=8), :]
        columns.append(column.reshape(256, 128).astype(jnp.bfloat16))
    lhs = jnp.concatenate(columns, 1)
    acc[...] += jnp.dot(lhs, rhs[...], preferred_element_type=jnp.float32)

    @pl.when(step == pl.num_programs(0) - 1)
    def _():
        first = jnp.where(section == 0, 1.0, 0.0)
        for slot in range(32):
            patch = slot // 16 * 4 + slot // 2 % 4
            rows = slice(8 * slot, 8 * slot + 8)
            acc[rows, :] += first * pos_ref[patch].astype(jnp.float32)
        out_ref[...] = acc[...].astype(jnp.bfloat16)


def embed(f, row, low, high, weight, pos, ids):
    taps, cols, channels, width = weight.shape
    members, rows, wide, _ = f.shape
    whole = lambda n: (lambda i, s: (0,) * n)
    return pl.pallas_call(
        embed_kernel,
        grid_spec=pltpu.PrefetchScalarGridSpec(
            num_scalar_prefetch=1,
            grid=(taps,),
            in_specs=[
                pl.BlockSpec(
                    (members, 8, 1, wide, channels),
                    lambda i, s: (0, 0, (i + 7 + 5 * s[0]) % 8, 0, 0),
                ),
                pl.BlockSpec(row.shape, whole(3)),
                pl.BlockSpec((1, 32, channels), lambda i, s: (i, 0, 0)),
                pl.BlockSpec((1, 32, channels), lambda i, s: (i, 0, 0)),
                pl.BlockSpec((1, cols, channels, width), lambda i, s: (i, 0, 0, 0)),
                pl.BlockSpec(pos.shape, whole(3)),
            ],
            out_specs=pl.BlockSpec((256, width), whole(2)),
            scratch_shapes=[
                pltpu.VMEM((32, 80, 128), jnp.float32),
                pltpu.VMEM((cols * 128, width), jnp.bfloat16),
                pltpu.VMEM((256, width), jnp.float32),
            ],
        ),
        out_shape=jax.ShapeDtypeStruct((256, width), jnp.bfloat16),
        compiler_params=pltpu.CompilerParams(vmem_limit_bytes=52 * 2**20),
        cost_estimate=pl.CostEstimate(
            flops=8 * 10**9, bytes_accessed=12 * 2**20, transcendentals=0
        ),
    )(ids, f.reshape(members, 8, rows // 8, wide, channels), row, low, high, weight, pos)


def attend_kernel(last, ids_ref, q_ref, kv_ref, kv2_ref, *refs):
    acc_refs, o_ref, v1 = refs[:-2], refs[-2], refs[-1]
    blocks, _, nk = kv_ref.shape
    bq = q_ref.shape[0]
    bk = 256

    @pl.when(pl.program_id(0) == 0)
    def _():
        for c in range(2 * blocks):
            rows = (kv_ref if c < blocks else kv2_ref)[c % blocks, HEAD:, :]
            stacked = jnp.concatenate([rows, jnp.ones_like(rows)], 0)
            v1[pl.ds(c * nk, nk), :] = stacked.T

    q = q_ref[...]

    def body(c, acc):
        for n, ref in enumerate((kv_ref, kv2_ref)):
            for b in range(0, nk, bk):
                scores = jnp.dot(q, ref[c, :HEAD, b : b + bk], preferred_element_type=jnp.float32)
                weights = jnp.exp2(scores).astype(jnp.bfloat16)
                at = pl.multiple_of((n * blocks + c) * nk + b, bk)
                values = v1[pl.ds(at, bk), :]
                acc = acc + jnp.dot(weights, values, preferred_element_type=jnp.float32)
        return acc

    if acc_refs:
        acc = acc_refs[0][...]
    else:
        acc = jnp.zeros((bq, 2 * HEAD), jnp.float32)
    acc = lax.fori_loop(0, blocks, body, acc)
    if last:
        halves = (acc / pltpu.roll(acc, HEAD, 1)).reshape(bq // 64, 2, 32, 2 * HEAD)
        left, right = halves[:, 0], halves[:, 1]
        right = pltpu.roll(right.reshape(bq // 2, 2 * HEAD), HEAD, 1).reshape(left.shape)
        lane = lax.broadcasted_iota(jnp.int32, left.shape, 2)
        packed = jnp.where(lane < HEAD, left, right).astype(jnp.bfloat16)
        half = packed.shape[0] // 2
        yh = ids_ref[3]
        o_ref[pl.ds(yh * half, half)] = packed[:half]
        o_ref[pl.ds(half - yh * half, half)] = packed[half:]
    else:
        o_ref[...] = acc


def attend(ids, q, kv, acc=None, last=False):
    n = q.shape[0]
    bq = n // CORE
    keys = 2 * kv[0].shape[0] * kv[0].shape[2]
    rows = lambda w: pl.BlockSpec((bq, w), lambda i, s: (i, 0))
    if last:
        out_spec = pl.BlockSpec((bq // 64, 32, 2 * HEAD), lambda i, s: ((i + s[1]) % CORE, 0, 0))
        out_shape = jax.ShapeDtypeStruct((n // 64, 32, 2 * HEAD), jnp.bfloat16)
    else:
        out_spec = rows(2 * HEAD)
        out_shape = jax.ShapeDtypeStruct((n, 2 * HEAD), jnp.float32)
    return pl.pallas_call(
        functools.partial(attend_kernel, last),
        grid_spec=pltpu.PrefetchScalarGridSpec(
            num_scalar_prefetch=1,
            grid=(CORE,),
            in_specs=[rows(HEAD)]
            + [pl.BlockSpec(a.shape, lambda i, s: (0, 0, 0)) for a in kv]
            + ([rows(2 * HEAD)] if acc is not None else []),
            out_specs=out_spec,
            scratch_shapes=[pltpu.VMEM((keys, 2 * HEAD), jnp.bfloat16)],
        ),
        out_shape=out_shape,
        compiler_params=pltpu.CompilerParams(vmem_limit_bytes=40 * 2**20),
        cost_estimate=pl.CostEstimate(
            flops=12 * n * keys * HEAD, bytes_accessed=4 * 2**20, transcendentals=n * keys
        ),
    )(ids, q, *kv, *([acc] if acc is not None else []))


def ring_z(own, beside, parts=1):
    z = lax.axis_index("z")
    rows, members, cols, width = own.shape
    size = rows // parts
    forward = [(i, (i + 1) % Z) for i in range(Z)]
    backward = [(target, source) for source, target in forward]
    out = jnp.zeros((rows, members, Z * cols, width), own.dtype)

    def place(out, shard, part, at):
        return lax.dynamic_update_slice(out, shard, (part * size, 0, (at % Z) * cols, 0))

    out = place(out, own, 0, z)
    ups = [own[p * size : (p + 1) * size] for p in range(parts)]
    downs = list(ups)
    for step in range(1, Z // 2 + 1):
        for p in range(parts):
            ups[p] = lax.ppermute(ups[p], "z", forward)
            if step < Z // 2:
                downs[p] = lax.ppermute(downs[p], "z", backward)
        if step == 2:
            ups, downs, beside = lax.optimization_barrier((ups, downs, beside))
        for p in range(parts):
            out = place(out, ups[p], p, z - step + Z)
            if step < Z // 2:
                out = place(out, downs[p], p, z + step)
    return out, beside


def project_kernel(ids_ref, x_ref, own_ref, other_ref, gain_ref, *out_refs):
    core = ids_ref[1]
    for rel_core in range(2):
        member = core if rel_core == 0 else 1 - core
        x = x_ref[:, member].reshape(-1, x_ref.shape[3])
        for rel_head, w in enumerate((own_ref[...], other_ref[: 3 * HEAD])):
            out = lax.dot_general(
                w, x, (((1,), (1,)), ((), ())), preferred_element_type=jnp.float32
            )
            out_ref = out_refs[2 * rel_core + rel_head]
            for kind in range(2):
                part = out[kind * HEAD : (kind + 1) * HEAD]
                mean = jnp.mean(part * part, axis=0, keepdims=True)
                part = part * lax.rsqrt(mean + head_epsilon) * gain_ref[rel_head, kind]
                if kind == 0:
                    part = part * (LOG2E / 8.0)
                out_ref[kind * HEAD : (kind + 1) * HEAD, :] = part.astype(jnp.bfloat16)
            out_ref[2 * HEAD :, :] = out[2 * HEAD :].astype(jnp.bfloat16)


def project(x, own, other, gains, ids):
    tokens = x.shape[0] * x.shape[2]
    whole = lambda a: pl.BlockSpec(a.shape, lambda i, s: (0,) * a.ndim)
    out = jax.ShapeDtypeStruct((3 * HEAD, tokens), jnp.bfloat16)
    return pl.pallas_call(
        project_kernel,
        grid_spec=pltpu.PrefetchScalarGridSpec(
            num_scalar_prefetch=1,
            grid=(1,),
            in_specs=[whole(x), whole(own), whole(other), whole(gains)],
            out_specs=[whole(out)] * 4,
        ),
        out_shape=[out] * 4,
        compiler_params=pltpu.CompilerParams(vmem_limit_bytes=32 * 2**20),
        cost_estimate=pl.CostEstimate(flops=3 * 10**9, bytes_accessed=4 * 2**20, transcendentals=0),
    )(ids, x, own, other, gains)


def mlp_kernel(ids_ref, x_ref, tok_ref, gu_ref, down_ref, other_ref, o_ref, acc):
    rows, members, cols, width = x_ref.shape
    units = down_ref.shape[0]
    x = x_ref[...].reshape(-1, width)
    contract = (((1,), (1,)), ((), ()))
    other = [other_ref[n * units : (n + 1) * units] for n in range(3)]
    total = None
    for gate_w, up_w, down_w in ((gu_ref[0], gu_ref[1], down_ref[...]), other):
        gate = lax.dot_general(x, gate_w, contract, preferred_element_type=jnp.float32)
        up = lax.dot_general(x, up_w, contract, preferred_element_type=jnp.float32)
        hidden = (gate / (1.0 + jnp.exp(-gate)) * up).astype(jnp.bfloat16)
        term = jnp.dot(hidden, down_w, preferred_element_type=jnp.float32)
        total = term if total is None else total + term
    acc[...] = total.reshape(acc.shape)
    at = pl.multiple_of(ids_ref[2] * 8, 8)
    acc[:, :, pl.ds(at, 8), :] += tok_ref[...].astype(jnp.float32)
    o_ref[...] = acc[...].astype(jnp.bfloat16)


def mlp(x, tokens, gu, down, other, ids, rows=4):
    whole = lambda a: pl.BlockSpec(a.shape, lambda i, s: (0,) * a.ndim)
    block = lambda a: pl.BlockSpec((rows,) + a.shape[1:], lambda i, s: (i, 0, 0, 0))
    return pl.pallas_call(
        mlp_kernel,
        grid_spec=pltpu.PrefetchScalarGridSpec(
            num_scalar_prefetch=1,
            grid=(x.shape[0] // rows,),
            in_specs=[block(x), block(tokens)] + [whole(a) for a in (gu, down, other)],
            out_specs=block(x),
            scratch_shapes=[pltpu.VMEM((rows,) + x.shape[1:], jnp.float32)],
        ),
        out_shape=jax.ShapeDtypeStruct(x.shape, jnp.bfloat16),
        compiler_params=pltpu.CompilerParams(vmem_limit_bytes=32 * 2**20),
        cost_estimate=pl.CostEstimate(flops=6 * 10**9, bytes_accessed=8 * 2**20, transcendentals=0),
    )(ids, x, tokens, gu, down, other)


def shards(
    fields,
    embed_weight,
    embed_bias,
    pos_embed,
    member_ids,
    member_table,
    norm_gain,
    w_qkv,
    query_gain,
    key_gain,
    w_gate_up,
    w_out,
    w_down,
):
    f32, bf16 = jnp.float32, jnp.bfloat16
    width = embed_weight.shape[3]
    yl = lax.axis_index("yl")
    yh = lax.axis_index("yh")
    core = lax.axis_index("core")

    gains = jnp.concatenate([query_gain, key_gain], 0)
    coarse = lax.reduce_precision(gains, 8, 7)
    middle = lax.reduce_precision(gains - coarse, 8, 7)
    fine = gains - coarse - middle
    terms = jnp.stack([coarse, middle, fine], 0).astype(bf16).reshape(1, 6 * HEAD)
    terms = jnp.pad(terms, ((0, 15), (0, width - 6 * HEAD)))
    qkv_other = other_half_weights(jnp.concatenate([w_qkv.reshape(-1, width), terms], 0))
    mlp_other = other_half_weights(
        jnp.concatenate([w_gate_up.reshape(-1, width), w_down], 0)
    )
    terms = qkv_other[-16:, : 6 * HEAD][0].astype(f32).reshape(3, 2, HEAD)
    gains_other = terms[0] + terms[1] + terms[2]
    gain_both = jnp.stack([gains, gains_other], 0)[..., None]
    ids = jnp.stack([yl, core, lax.axis_index("z"), yh]).astype(jnp.int32)

    f = jnp.transpose(fields, (0, 2, 3, 1))
    row, low, high = halo(f, ids, yl)
    part = embed(f, row, low, high, embed_weight, pos_embed, ids)
    part = lax.all_to_all(part, ("yh", "yl"), 0, 0, tiled=True)
    part = part.reshape(YH, YL, 4, 2, 8, width).astype(f32)
    embedded = jnp.transpose(part[:, 0] + part[:, 1], (1, 0, 2, 3, 4)).reshape(8, 2, 8, width)
    one_hot = (
        member_ids[:, None] == jnp.arange(member_table.shape[0], dtype=jnp.int32)[None, :]
    ).astype(bf16)
    member_vecs = jnp.dot(one_hot, member_table, preferred_element_type=f32)
    tokens = (
        embedded
        + embed_bias.astype(f32)
        + member_vecs[None, :, None, :]
    ).astype(bf16)
    residual = tokens.astype(f32)
    average = jnp.mean(residual, axis=-1, keepdims=True)
    centered = residual - average
    variance = jnp.mean(centered * centered, axis=-1, keepdims=True)
    normed = (centered * lax.rsqrt(variance + layer_epsilon) * norm_gain).astype(bf16)

    normed_all, qkv_other = ring_z(normed, qkv_other)
    normed_all, mlp_other, w_out = lax.optimization_barrier((normed_all, mlp_other, w_out))
    w_out_half = lax.all_gather(w_out, "z", axis=0, tiled=True)

    mine, mine_yh, theirs, theirs_yh = project(
        normed_all, w_qkv.reshape(3 * HEAD, width), qkv_other, gain_both, ids
    )
    pair = ("core", "yh")
    got_core = lax.ppermute(theirs, pair, [(0, 2), (2, 0), (1, 3), (3, 1)])
    got_yh = lax.ppermute(mine_yh, pair, [(0, 1), (1, 0), (2, 3), (3, 2)])
    got_both = lax.ppermute(theirs_yh, pair, [(0, 3), (3, 0), (1, 2), (2, 1)])

    update = mlp(normed_all, tokens, w_gate_up, w_down, mlp_other, ids)
    got_core, got_yh, got_both, update = lax.optimization_barrier(
        (got_core, got_yh, got_both, update)
    )
    summed = lax.psum_scatter(update, "z", scatter_dimension=0, tiled=True)[0]
    first = jnp.stack([mine[HEAD:], got_yh[HEAD:]], 0)
    second = jnp.stack([got_core[HEAD:], got_both[HEAD:]], 0)
    q = jnp.stack([a[:HEAD] for a in (mine, got_yh, got_core, got_both)], 0)
    q = jnp.transpose(q, (0, 2, 1)).reshape(-1, HEAD)

    x_up = [(i, (i + 1) % X) for i in range(X)]
    x_down = [(target, source) for source, target in x_up]
    near = [lax.ppermute(first, "x", x_up), lax.ppermute(second, "x", x_down)]
    late = [lax.ppermute(second, "x", x_up), lax.ppermute(first, "x", x_down)]
    far = [lax.ppermute(near[0], "x", x_up), lax.ppermute(near[1], "x", x_down)]

    acc = attend(ids, q, (first, second))
    acc = attend(ids, q, near, acc)
    acc = attend(ids, q, late, acc)
    acc, w_out_half = lax.optimization_barrier((acc, w_out_half))
    w_out_other = other_half_weights(w_out_half)
    attended = attend(ids, q, far, acc, last=True)
    attended = lax.all_to_all(attended, ("core", "yh", "z"), 0, 0, tiled=True)
    attended = attended.reshape(CORE, YH, Z, 32, 2, HEAD)
    attended = jnp.transpose(attended, (0, 4, 3, 1, 2, 5)).reshape(CORE * 64, YH * Z * HEAD)
    half = Z * HEAD
    own_cols = lax.dynamic_slice_in_dim(attended, yh * half, half, 1)
    other_cols = lax.dynamic_slice_in_dim(attended, half - yh * half, half, 1)
    mixed = jnp.dot(own_cols, w_out_half, preferred_element_type=f32)
    mixed = mixed + jnp.dot(other_cols, w_out_other, preferred_element_type=f32)
    mixed = mixed.reshape(2, 64, width)
    return (summed.astype(f32) + mixed).astype(bf16)


def solution(mesh):
    chips = Mesh(mesh.devices.reshape(X, CORE, YH, Z, YL), ("x", "core", "yh", "z", "yl"))
    return jax.shard_map(
        shards,
        mesh=chips,
        in_specs=(
            P(None, None, LAT, LON),
            P("yl", None, None, None),
            P(),
            P(LAT, LON, None),
            P("yl"),
            P(),
            P(),
            P(None, LON, None),
            P(LON, None),
            P(LON, None),
            P(None, LON, None),
            P(LON, None),
            P(LON, None),
        ),
        out_specs=P("yl", LAT + LON, None),
        check_vma=False,
    )
```

```python
import functools

import jax
import jax.numpy as jnp
from jax import lax
from jax.experimental import pallas as pl
from jax.experimental.pallas import tpu as pltpu
from jax.sharding import Mesh, PartitionSpec as P

PATCH = 8
layer_epsilon = 1e-05
head_epsilon = 1e-06
LOG2E = 1.4426950408889634
HEAD = 64

X, CORE, YH, Z, YL = 4, 2, 2, 8, 2
LAT = ("x", "core")
LON = ("yh", "z")


def other_half_weights(array):
    return lax.ppermute(array, ("yh", "yl"), [(0, 3), (3, 0), (1, 2), (2, 1)])


def edges_kernel(s_ref, top_ref, left_ref, right_ref, row_ref, low_ref, high_ref, wide):
    row_ref[...] = top_ref[:, 0]
    members, rows, cols, channels = right_ref.shape
    wide[..., :channels] = right_ref[...].reshape(wide.shape[0], cols, channels).astype(jnp.float32)
    low = wide[:, cols - 1, :channels]
    low_ref[...] = low.reshape(low_ref.shape).astype(jnp.bfloat16)
    wide[..., :channels] = left_ref[...].reshape(wide.shape[0], cols, channels).astype(jnp.float32)
    high = wide[:, 0, :channels]
    high_ref[...] = high.reshape(high_ref.shape).astype(jnp.bfloat16)


def edges(f, ids):
    members, rows, cols, channels = f.shape
    column = (members, rows, 16, channels)
    line = jax.ShapeDtypeStruct((members, rows, channels), f.dtype)
    whole = pl.BlockSpec((members, rows, channels), lambda i, s: (0, 0, 0))
    return pl.pallas_call(
        edges_kernel,
        grid_spec=pltpu.PrefetchScalarGridSpec(
            num_scalar_prefetch=1,
            grid=(1,),
            in_specs=[
                pl.BlockSpec(
                    (members, 1, cols, channels), lambda i, s: (0, (1 - s[0]) * (rows - 1), 0, 0)
                ),
                pl.BlockSpec(column, lambda i, s: (0, 0, 0, 0)),
                pl.BlockSpec(column, lambda i, s: (0, 0, cols // 16 - 1, 0)),
            ],
            out_specs=[whole] * 3,
            scratch_shapes=[pltpu.VMEM((members * rows, 16, 128), jnp.float32)],
        ),
        out_shape=[line] * 3,
        compiler_params=pltpu.CompilerParams(vmem_limit_bytes=40 * 2**20),
    )(ids, f, f, f)


def halo(f, ids, section):
    lats, lons = X * CORE, YH * Z
    row, low, high = edges(f, ids)
    to_lat = [(2 * i, 2 * i + 2) for i in range(lats - 1)]
    to_lat += [(2 * i + 1, 2 * i - 1) for i in range(1, lats)]
    forward = [(i, (i + 1) % lons) for i in range(lons)]
    backward = [(target, source) for source, target in forward]
    row = lax.ppermute(row, LAT + ("yl",), to_lat)

    def column(edge, corner, pairs):
        edge = jnp.concatenate([edge, corner[:, None]], 1)
        edge = lax.ppermute(edge, LON, pairs)
        edge = jnp.concatenate([edge[:, -1:], edge, jnp.zeros_like(edge[:, :3])], 1)
        edge = lax.dynamic_slice_in_dim(edge, section * 5, 64, 1)
        edge = edge.reshape(2, 2, 2, 4, 8, edge.shape[-1])[:, :, :, :, :5].astype(jnp.float32)
        return jnp.transpose(edge, (4, 2, 0, 3, 1, 5)).reshape(5, 32, edge.shape[-1])

    return row, column(low, row[:, -1], forward), column(high, row[:, 0], backward)


def embed_kernel(
    ids_ref, f_ref, row_ref, low_ref, high_ref, w_ref, pos_ref, out_ref, xf, rhs, acc
):
    step = pl.program_id(0)
    section = ids_ref[0]
    channels = f_ref.shape[4]
    offset = step - 1 + 5 * section
    shift = jnp.where(offset < 0, -1, jnp.where(offset > 7, 1, 0))

    @pl.when(step == 0)
    def _():
        xf[...] = jnp.zeros_like(xf)
        rhs[...] = jnp.zeros_like(rhs)
        acc[...] = jnp.zeros_like(acc)

    for slot in range(32):
        patch = slot // 16 * 4 + slot // 2 % 4
        member = slot // 8 % 2 * 2 + slot % 2
        at = patch + shift
        value = f_ref[member, jnp.clip(at, 0, 7), 0]
        if patch in (0, 7):
            value = jnp.where((at < 0) | (at > 7), row_ref[member], value)
        xf[slot, 8:72, :channels] = value.astype(jnp.float32)
        xf[slot, 7:8, :channels] = low_ref[0, slot : slot + 1]
        xf[slot, 72:73, :channels] = high_ref[0, slot : slot + 1]
    taps = w_ref.shape[1]
    columns = []
    for b in range(taps):
        rhs[b * 128 : b * 128 + channels, :] = w_ref[0, b]
        column = xf[:, pl.ds(7 + b, 8, stride=8), :]
        columns.append(column.reshape(256, 128).astype(jnp.bfloat16))
    lhs = jnp.concatenate(columns, 1)
    acc[...] += jnp.dot(lhs, rhs[...], preferred_element_type=jnp.float32)

    @pl.when(step == pl.num_programs(0) - 1)
    def _():
        first = jnp.where(section == 0, 1.0, 0.0)
        for slot in range(32):
            patch = slot // 16 * 4 + slot // 2 % 4
            rows = slice(8 * slot, 8 * slot + 8)
            acc[rows, :] += first * pos_ref[patch].astype(jnp.float32)
        out_ref[...] = acc[...].astype(jnp.bfloat16)


def embed(f, row, low, high, weight, pos, ids):
    taps, cols, channels, width = weight.shape
    members, rows, wide, _ = f.shape
    whole = lambda n: (lambda i, s: (0,) * n)
    return pl.pallas_call(
        embed_kernel,
        grid_spec=pltpu.PrefetchScalarGridSpec(
            num_scalar_prefetch=1,
            grid=(taps,),
            in_specs=[
                pl.BlockSpec(
                    (members, 8, 1, wide, channels),
                    lambda i, s: (0, 0, (i + 7 + 5 * s[0]) % 8, 0, 0),
                ),
                pl.BlockSpec(row.shape, whole(3)),
                pl.BlockSpec((1, 32, channels), lambda i, s: (i, 0, 0)),
                pl.BlockSpec((1, 32, channels), lambda i, s: (i, 0, 0)),
                pl.BlockSpec((1, cols, channels, width), lambda i, s: (i, 0, 0, 0)),
                pl.BlockSpec(pos.shape, whole(3)),
            ],
            out_specs=pl.BlockSpec((256, width), whole(2)),
            scratch_shapes=[
                pltpu.VMEM((32, 80, 128), jnp.float32),
                pltpu.VMEM((cols * 128, width), jnp.bfloat16),
                pltpu.VMEM((256, width), jnp.float32),
            ],
        ),
        out_shape=jax.ShapeDtypeStruct((256, width), jnp.bfloat16),
        compiler_params=pltpu.CompilerParams(vmem_limit_bytes=52 * 2**20),
        cost_estimate=pl.CostEstimate(
            flops=8 * 10**9, bytes_accessed=12 * 2**20, transcendentals=0
        ),
    )(ids, f.reshape(members, 8, rows // 8, wide, channels), row, low, high, weight, pos)


def attend_kernel(last, ids_ref, q_ref, kv_ref, kv2_ref, *refs):
    acc_refs, o_ref, v1 = refs[:-2], refs[-2], refs[-1]
    blocks, _, nk = kv_ref.shape
    bq = q_ref.shape[0]
    bk = 256

    @pl.when(pl.program_id(0) == 0)
    def _():
        for c in range(2 * blocks):
            rows = (kv_ref if c < blocks else kv2_ref)[c % blocks, HEAD:, :]
            stacked = jnp.concatenate([rows, jnp.ones_like(rows)], 0)
            v1[pl.ds(c * nk, nk), :] = stacked.T

    q = q_ref[...]

    def body(c, acc):
        for n, ref in enumerate((kv_ref, kv2_ref)):
            for b in range(0, nk, bk):
                scores = jnp.dot(q, ref[c, :HEAD, b : b + bk], preferred_element_type=jnp.float32)
                weights = jnp.exp2(scores).astype(jnp.bfloat16)
                at = (n * blocks + c) * nk + b
                values = v1[at : at + bk, :]
                acc = acc + jnp.dot(weights, values, preferred_element_type=jnp.float32)
        return acc

    if acc_refs:
        acc = acc_refs[0][...]
    else:
        acc = jnp.zeros((bq, 2 * HEAD), jnp.float32)
    for c in range(blocks):
        acc = body(c, acc)
    if last:
        halves = (acc / pltpu.roll(acc, HEAD, 1)).reshape(bq // 64, 2, 32, 2 * HEAD)
        left, right = halves[:, 0], halves[:, 1]
        right = pltpu.roll(right.reshape(bq // 2, 2 * HEAD), HEAD, 1).reshape(left.shape)
        lane = lax.broadcasted_iota(jnp.int32, left.shape, 2)
        packed = jnp.where(lane < HEAD, left, right).astype(jnp.bfloat16)
        half = packed.shape[0] // 2
        yh = ids_ref[3]
        o_ref[pl.ds(yh * half, half)] = packed[:half]
        o_ref[pl.ds(half - yh * half, half)] = packed[half:]
    else:
        o_ref[...] = acc


def attend(ids, q, kv, acc=None, last=False):
    n = q.shape[0]
    bq = n // CORE
    keys = 2 * kv[0].shape[0] * kv[0].shape[2]
    rows = lambda w: pl.BlockSpec((bq, w), lambda i, s: (i, 0))
    if last:
        out_spec = pl.BlockSpec((bq // 64, 32, 2 * HEAD), lambda i, s: ((i + s[1]) % CORE, 0, 0))
        out_shape = jax.ShapeDtypeStruct((n // 64, 32, 2 * HEAD), jnp.bfloat16)
    else:
        out_spec = rows(2 * HEAD)
        out_shape = jax.ShapeDtypeStruct((n, 2 * HEAD), jnp.float32)
    return pl.pallas_call(
        functools.partial(attend_kernel, last),
        grid_spec=pltpu.PrefetchScalarGridSpec(
            num_scalar_prefetch=1,
            grid=(CORE,),
            in_specs=[rows(HEAD)]
            + [pl.BlockSpec(a.shape, lambda i, s: (0, 0, 0)) for a in kv]
            + ([rows(2 * HEAD)] if acc is not None else []),
            out_specs=out_spec,
            scratch_shapes=[pltpu.VMEM((keys, 2 * HEAD), jnp.bfloat16)],
        ),
        out_shape=out_shape,
        compiler_params=pltpu.CompilerParams(vmem_limit_bytes=40 * 2**20),
        cost_estimate=pl.CostEstimate(
            flops=12 * n * keys * HEAD, bytes_accessed=4 * 2**20, transcendentals=n * keys
        ),
    )(ids, q, *kv, *([acc] if acc is not None else []))


def ring_z(own, beside, parts=1):
    z = lax.axis_index("z")
    rows, members, cols, width = own.shape
    size = rows // parts
    forward = [(i, (i + 1) % Z) for i in range(Z)]
    backward = [(target, source) for source, target in forward]
    out = jnp.zeros((rows, members, Z * cols, width), own.dtype)

    def place(out, shard, part, at):
        return lax.dynamic_update_slice(out, shard, (part * size, 0, (at % Z) * cols, 0))

    out = place(out, own, 0, z)
    ups = [own[p * size : (p + 1) * size] for p in range(parts)]
    downs = list(ups)
    for step in range(1, Z // 2 + 1):
        for p in range(parts):
            ups[p] = lax.ppermute(ups[p], "z", forward)
            if step < Z // 2:
                downs[p] = lax.ppermute(downs[p], "z", backward)
        if step == 2:
            ups, downs, beside = lax.optimization_barrier((ups, downs, beside))
        for p in range(parts):
            out = place(out, ups[p], p, z - step + Z)
            if step < Z // 2:
                out = place(out, downs[p], p, z + step)
    return out, beside


def project_kernel(ids_ref, x_ref, own_ref, other_ref, gain_ref, *out_refs):
    core = ids_ref[1]
    for rel_core in range(2):
        member = core if rel_core == 0 else 1 - core
        x = x_ref[:, member].reshape(-1, x_ref.shape[3])
        for rel_head, w in enumerate((own_ref[...], other_ref[: 3 * HEAD])):
            out = lax.dot_general(
                w, x, (((1,), (1,)), ((), ())), preferred_element_type=jnp.float32
            )
            out_ref = out_refs[2 * rel_core + rel_head]
            for kind in range(2):
                part = out[kind * HEAD : (kind + 1) * HEAD]
                mean = jnp.mean(part * part, axis=0, keepdims=True)
                part = part * lax.rsqrt(mean + head_epsilon) * gain_ref[rel_head, kind]
                if kind == 0:
                    part = part * (LOG2E / 8.0)
                out_ref[kind * HEAD : (kind + 1) * HEAD, :] = part.astype(jnp.bfloat16)
            out_ref[2 * HEAD :, :] = out[2 * HEAD :].astype(jnp.bfloat16)


def project(x, own, other, gains, ids):
    tokens = x.shape[0] * x.shape[2]
    whole = lambda a: pl.BlockSpec(a.shape, lambda i, s: (0,) * a.ndim)
    out = jax.ShapeDtypeStruct((3 * HEAD, tokens), jnp.bfloat16)
    return pl.pallas_call(
        project_kernel,
        grid_spec=pltpu.PrefetchScalarGridSpec(
            num_scalar_prefetch=1,
            grid=(1,),
            in_specs=[whole(x), whole(own), whole(other), whole(gains)],
            out_specs=[whole(out)] * 4,
        ),
        out_shape=[out] * 4,
        compiler_params=pltpu.CompilerParams(vmem_limit_bytes=32 * 2**20),
        cost_estimate=pl.CostEstimate(flops=3 * 10**9, bytes_accessed=4 * 2**20, transcendentals=0),
    )(ids, x, own, other, gains)


def mlp_kernel(ids_ref, x_ref, tok_ref, gu_ref, down_ref, some_ref, rest_ref, o_ref, acc):
    rows, members, cols, width = x_ref.shape
    units = down_ref.shape[0] // 2
    x = x_ref[...].reshape(-1, width)
    contract = (((1,), (1,)), ((), ()))
    other = []
    for n in range(3):
        rows_n = slice(n * units, (n + 1) * units)
        other.append(jnp.concatenate([some_ref[rows_n], rest_ref[rows_n]], 0))
    total = None
    for gate_w, up_w, down_w in ((gu_ref[0], gu_ref[1], down_ref[...]), other):
        gate = lax.dot_general(x, gate_w, contract, preferred_element_type=jnp.float32)
        up = lax.dot_general(x, up_w, contract, preferred_element_type=jnp.float32)
        hidden = (gate / (1.0 + jnp.exp(-gate)) * up).astype(jnp.bfloat16)
        term = jnp.dot(hidden, down_w, preferred_element_type=jnp.float32)
        total = term if total is None else total + term
    acc[...] = total.reshape(acc.shape)
    at = pl.multiple_of(ids_ref[2] * 8, 8)
    acc[:, :, pl.ds(at, 8), :] += tok_ref[...].astype(jnp.float32)
    o_ref[...] = acc[...].astype(jnp.bfloat16)


def mlp(x, tokens, gu, down, some, rest, ids, rows=4):
    whole = lambda a: pl.BlockSpec(a.shape, lambda i, s: (0,) * a.ndim)
    block = lambda a: pl.BlockSpec((rows,) + a.shape[1:], lambda i, s: (i, 0, 0, 0))
    return pl.pallas_call(
        mlp_kernel,
        grid_spec=pltpu.PrefetchScalarGridSpec(
            num_scalar_prefetch=1,
            grid=(x.shape[0] // rows,),
            in_specs=[block(x), block(tokens)] + [whole(a) for a in (gu, down, some, rest)],
            out_specs=block(x),
            scratch_shapes=[pltpu.VMEM((rows,) + x.shape[1:], jnp.float32)],
        ),
        out_shape=jax.ShapeDtypeStruct(x.shape, jnp.bfloat16),
        compiler_params=pltpu.CompilerParams(vmem_limit_bytes=32 * 2**20),
        cost_estimate=pl.CostEstimate(flops=6 * 10**9, bytes_accessed=8 * 2**20, transcendentals=0),
    )(ids, x, tokens, gu, down, some, rest)


def shards(
    fields,
    embed_weight,
    embed_bias,
    pos_embed,
    member_ids,
    member_table,
    norm_gain,
    w_qkv,
    query_gain,
    key_gain,
    w_gate_up,
    w_out,
    w_down,
):
    f32, bf16 = jnp.float32, jnp.bfloat16
    width = embed_weight.shape[3]
    yl = lax.axis_index("yl")
    yh = lax.axis_index("yh")
    core = lax.axis_index("core")

    gains = jnp.concatenate([query_gain, key_gain], 0)
    coarse = lax.reduce_precision(gains, 8, 7)
    middle = lax.reduce_precision(gains - coarse, 8, 7)
    fine = gains - coarse - middle
    terms = jnp.stack([coarse, middle, fine], 0).astype(bf16).reshape(1, 6 * HEAD)
    terms = jnp.pad(terms, ((0, 15), (0, width - 6 * HEAD)))
    ids = jnp.stack([yl, core, lax.axis_index("z"), yh]).astype(jnp.int32)

    f = jnp.transpose(fields, (0, 2, 3, 1))
    row, low, high = halo(f, ids, yl)
    part = embed(f, row, low, high, embed_weight, pos_embed, ids)
    part = lax.all_to_all(part, ("yh", "yl"), 0, 0, tiled=True)
    part, terms, w_qkv, w_gate_up, w_down = lax.optimization_barrier(
        (part, terms, w_qkv, w_gate_up, w_down)
    )
    qkv_other = other_half_weights(jnp.concatenate([w_qkv.reshape(-1, width), terms], 0))
    units = w_down.shape[0] // 2
    some_gu = lax.dynamic_slice_in_dim(w_gate_up, core * units, units, 1)
    some_down = lax.dynamic_slice_in_dim(w_down, core * units, units, 0)
    mlp_other = other_half_weights(
        jnp.concatenate([some_gu.reshape(-1, width), some_down], 0)
    )
    terms = qkv_other[-16:, : 6 * HEAD][0].astype(f32).reshape(3, 2, HEAD)
    gains_other = terms[0] + terms[1] + terms[2]
    gain_both = jnp.stack([gains, gains_other], 0)[..., None]
    part = part.reshape(YH, YL, 4, 2, 8, width).astype(f32)
    embedded = jnp.transpose(part[:, 0] + part[:, 1], (1, 0, 2, 3, 4)).reshape(8, 2, 8, width)
    one_hot = (
        member_ids[:, None] == jnp.arange(member_table.shape[0], dtype=jnp.int32)[None, :]
    ).astype(bf16)
    member_vecs = jnp.dot(one_hot, member_table, preferred_element_type=f32)
    tokens = (
        embedded
        + embed_bias.astype(f32)
        + member_vecs[None, :, None, :]
    ).astype(bf16)
    residual = tokens.astype(f32)
    average = jnp.mean(residual, axis=-1, keepdims=True)
    centered = residual - average
    variance = jnp.mean(centered * centered, axis=-1, keepdims=True)
    normed = (centered * lax.rsqrt(variance + layer_epsilon) * norm_gain).astype(bf16)

    normed_all, qkv_other = ring_z(normed, qkv_other)
    normed_all, mlp_other, w_out = lax.optimization_barrier((normed_all, mlp_other, w_out))
    w_out_half = lax.all_gather(w_out, "z", axis=0, tiled=True)

    mine, mine_yh, theirs, theirs_yh = project(
        normed_all, w_qkv.reshape(3 * HEAD, width), qkv_other, gain_both, ids
    )
    pair = ("core", "yh")
    got_core = lax.ppermute(theirs, pair, [(0, 2), (2, 0), (1, 3), (3, 1)])
    got_yh = lax.ppermute(mine_yh, pair, [(0, 1), (1, 0), (2, 3), (3, 2)])
    got_both = lax.ppermute(theirs_yh, pair, [(0, 3), (3, 0), (1, 2), (2, 1)])

    mlp_rest = lax.ppermute(mlp_other, "core", [(0, 1), (1, 0)])
    update = mlp(normed_all, tokens, w_gate_up, w_down, mlp_other, mlp_rest, ids)
    got_core, got_yh, got_both, update = lax.optimization_barrier(
        (got_core, got_yh, got_both, update)
    )
    summed = lax.psum_scatter(update, "z", scatter_dimension=0, tiled=True)[0]
    first = jnp.stack([mine[HEAD:], got_yh[HEAD:]], 0)
    second = jnp.stack([got_core[HEAD:], got_both[HEAD:]], 0)
    q = jnp.stack([a[:HEAD] for a in (mine, got_yh, got_core, got_both)], 0)
    q = jnp.transpose(q, (0, 2, 1)).reshape(-1, HEAD)

    x_up = [(i, (i + 1) % X) for i in range(X)]
    x_down = [(target, source) for source, target in x_up]
    near = [lax.ppermute(first, "x", x_up), lax.ppermute(second, "x", x_down)]
    late = [lax.ppermute(second, "x", x_up), lax.ppermute(first, "x", x_down)]
    far = [lax.ppermute(near[0], "x", x_up), lax.ppermute(near[1], "x", x_down)]

    acc = attend(ids, q, (first, second))
    acc = attend(ids, q, near, acc)
    acc = attend(ids, q, late, acc)
    acc, w_out_half = lax.optimization_barrier((acc, w_out_half))
    w_out_other = other_half_weights(w_out_half)
    attended = attend(ids, q, far, acc, last=True)
    attended = lax.all_to_all(attended, ("core", "yh", "z"), 0, 0, tiled=True)
    attended = attended.reshape(CORE, YH, Z, 32, 2, HEAD)
    attended = jnp.transpose(attended, (0, 4, 3, 1, 2, 5)).reshape(CORE * 64, YH * Z * HEAD)
    half = Z * HEAD
    own_cols = lax.dynamic_slice_in_dim(attended, yh * half, half, 1)
    other_cols = lax.dynamic_slice_in_dim(attended, half - yh * half, half, 1)
    mixed = jnp.dot(own_cols, w_out_half, preferred_element_type=f32)
    mixed = mixed + jnp.dot(other_cols, w_out_other, preferred_element_type=f32)
    mixed = mixed.reshape(2, 64, width)
    return (summed.astype(f32) + mixed).astype(bf16)


def solution(mesh):
    chips = Mesh(mesh.devices.reshape(X, CORE, YH, Z, YL), ("x", "core", "yh", "z", "yl"))
    return jax.shard_map(
        shards,
        mesh=chips,
        in_specs=(
            P(None, None, LAT, LON),
            P("yl", None, None, None),
            P(),
            P(LAT, LON, None),
            P("yl"),
            P(),
            P(),
            P(None, LON, None),
            P(LON, None),
            P(LON, None),
            P(None, LON, None),
            P(LON, None),
            P(LON, None),
        ),
        out_specs=P("yl", LAT + LON, None),
        check_vma=False,
    )
```

```python
import functools

import jax
import jax.numpy as jnp
from jax import lax
from jax.experimental import pallas as pl
from jax.experimental.pallas import tpu as pltpu
from jax.sharding import Mesh, PartitionSpec as P

PATCH = 8
layer_epsilon = 1e-05
head_epsilon = 1e-06
LOG2E = 1.4426950408889634
HEAD = 64

X, CORE, YH, Z, YL = 4, 2, 2, 8, 2
LAT = ("x", "core")
LON = ("yh", "z")


def other_half_weights(array):
    return lax.ppermute(array, ("yh", "yl"), [(0, 3), (3, 0), (1, 2), (2, 1)])


def edges_kernel(s_ref, top_ref, left_ref, right_ref, row_ref, low_ref, high_ref, wide):
    row_ref[...] = top_ref[:, 0]
    members, rows, cols, channels = right_ref.shape
    wide[..., :channels] = right_ref[...].reshape(wide.shape[0], cols, channels).astype(jnp.float32)
    low = wide[:, cols - 1, :channels]
    low_ref[...] = low.reshape(low_ref.shape).astype(jnp.bfloat16)
    wide[..., :channels] = left_ref[...].reshape(wide.shape[0], cols, channels).astype(jnp.float32)
    high = wide[:, 0, :channels]
    high_ref[...] = high.reshape(high_ref.shape).astype(jnp.bfloat16)


def edges(f, ids):
    members, rows, cols, channels = f.shape
    column = (members, rows, 16, channels)
    line = jax.ShapeDtypeStruct((members, rows, channels), f.dtype)
    whole = pl.BlockSpec((members, rows, channels), lambda i, s: (0, 0, 0))
    return pl.pallas_call(
        edges_kernel,
        grid_spec=pltpu.PrefetchScalarGridSpec(
            num_scalar_prefetch=1,
            grid=(1,),
            in_specs=[
                pl.BlockSpec(
                    (members, 1, cols, channels), lambda i, s: (0, (1 - s[0]) * (rows - 1), 0, 0)
                ),
                pl.BlockSpec(column, lambda i, s: (0, 0, 0, 0)),
                pl.BlockSpec(column, lambda i, s: (0, 0, cols // 16 - 1, 0)),
            ],
            out_specs=[whole] * 3,
            scratch_shapes=[pltpu.VMEM((members * rows, 16, 128), jnp.float32)],
        ),
        out_shape=[line] * 3,
        compiler_params=pltpu.CompilerParams(vmem_limit_bytes=40 * 2**20),
    )(ids, f, f, f)


def halo(f, ids, section):
    lats, lons = X * CORE, YH * Z
    row, low, high = edges(f, ids)
    to_lat = [(2 * i, 2 * i + 2) for i in range(lats - 1)]
    to_lat += [(2 * i + 1, 2 * i - 1) for i in range(1, lats)]
    forward = [(i, (i + 1) % lons) for i in range(lons)]
    backward = [(target, source) for source, target in forward]
    row = lax.ppermute(row, LAT + ("yl",), to_lat)

    def column(edge, corner, pairs):
        edge = jnp.concatenate([edge, corner[:, None]], 1)
        edge = lax.ppermute(edge, LON, pairs)
        edge = jnp.concatenate([edge[:, -1:], edge, jnp.zeros_like(edge[:, :3])], 1)
        edge = lax.dynamic_slice_in_dim(edge, section * 5, 64, 1)
        edge = edge.reshape(2, 2, 2, 4, 8, edge.shape[-1])[:, :, :, :, :5].astype(jnp.float32)
        return jnp.transpose(edge, (4, 2, 0, 3, 1, 5)).reshape(5, 32, edge.shape[-1])

    return row, column(low, row[:, -1], forward), column(high, row[:, 0], backward)


def embed_kernel(
    ids_ref, f_ref, row_ref, low_ref, high_ref, w_ref, w2_ref, pos_ref, out_ref, xf, rhs, acc
):
    step = pl.program_id(0)
    section = ids_ref[0]
    channels = f_ref.shape[4]
    offset = step - 1 + 5 * section
    shift = jnp.where(offset < 0, -1, jnp.where(offset > 7, 1, 0))

    @pl.when(step == 0)
    def _():
        xf[...] = jnp.zeros_like(xf)
        rhs[...] = jnp.zeros_like(rhs)
        acc[...] = jnp.zeros_like(acc)

    for slot in range(32):
        patch = slot // 16 * 4 + slot // 2 % 4
        member = slot // 8 % 2 * 2 + slot % 2
        at = patch + shift
        value = f_ref[member, jnp.clip(at, 0, 7), 0]
        if patch in (0, 7):
            value = jnp.where((at < 0) | (at > 7), row_ref[member], value)
        xf[slot, 8:72, :channels] = value.astype(jnp.float32)
        xf[slot, 7:8, :channels] = low_ref[0, slot : slot + 1]
        xf[slot, 72:73, :channels] = high_ref[0, slot : slot + 1]
    half = w_ref.shape[1]
    columns = []
    for b in range(2 * half):
        rhs[b * 128 : b * 128 + channels, :] = (w_ref if b < half else w2_ref)[0, b % half]
        column = xf[:, pl.ds(7 + b, 8, stride=8), :]
        columns.append(column.reshape(256, 128).astype(jnp.bfloat16))
    lhs = jnp.concatenate(columns, 1)
    acc[...] += jnp.dot(lhs, rhs[...], preferred_element_type=jnp.float32)

    @pl.when(step == pl.num_programs(0) - 1)
    def _():
        first = jnp.where(section == 0, 1.0, 0.0)
        for slot in range(32):
            patch = slot // 16 * 4 + slot // 2 % 4
            rows = slice(8 * slot, 8 * slot + 8)
            acc[rows, :] += first * pos_ref[patch].astype(jnp.float32)
        out_ref[...] = acc[...].astype(jnp.bfloat16)


def embed(f, row, low, high, weight, pos, ids):
    taps, cols, channels, width = weight.shape
    members, rows, wide, _ = f.shape
    whole = lambda n: (lambda i, s: (0,) * n)
    return pl.pallas_call(
        embed_kernel,
        grid_spec=pltpu.PrefetchScalarGridSpec(
            num_scalar_prefetch=1,
            grid=(taps,),
            in_specs=[
                pl.BlockSpec(
                    (members, 8, 1, wide, channels),
                    lambda i, s: (0, 0, (i + 7 + 5 * s[0]) % 8, 0, 0),
                ),
                pl.BlockSpec(row.shape, whole(3)),
                pl.BlockSpec((1, 32, channels), lambda i, s: (i, 0, 0)),
                pl.BlockSpec((1, 32, channels), lambda i, s: (i, 0, 0)),
                pl.BlockSpec((1, cols // 2, channels, width), lambda i, s: (i, 0, 0, 0)),
                pl.BlockSpec((1, cols // 2, channels, width), lambda i, s: (i, 1, 0, 0)),
                pl.BlockSpec(pos.shape, whole(3)),
            ],
            out_specs=pl.BlockSpec((256, width), whole(2)),
            scratch_shapes=[
                pltpu.VMEM((32, 80, 128), jnp.float32),
                pltpu.VMEM((cols * 128, width), jnp.bfloat16),
                pltpu.VMEM((256, width), jnp.float32),
            ],
        ),
        out_shape=jax.ShapeDtypeStruct((256, width), jnp.bfloat16),
        compiler_params=pltpu.CompilerParams(vmem_limit_bytes=52 * 2**20),
        cost_estimate=pl.CostEstimate(
            flops=8 * 10**9, bytes_accessed=12 * 2**20, transcendentals=0
        ),
    )(ids, f.reshape(members, 8, rows // 8, wide, channels), row, low, high, weight, weight, pos)


def attend_kernel(last, ids_ref, q_ref, kv_ref, kv2_ref, *refs):
    acc_refs, o_ref, v1 = refs[:-2], refs[-2], refs[-1]
    blocks, _, nk = kv_ref.shape
    bq = q_ref.shape[0]
    bk = 256

    @pl.when(pl.program_id(0) == 0)
    def _():
        for c in range(2 * blocks):
            rows = (kv_ref if c < blocks else kv2_ref)[c % blocks, HEAD:, :]
            stacked = jnp.concatenate([rows, jnp.ones_like(rows)], 0)
            v1[pl.ds(c * nk, nk), :] = stacked.T

    q = q_ref[...]

    def body(c, acc):
        for n, ref in enumerate((kv_ref, kv2_ref)):
            for b in range(0, nk, bk):
                scores = jnp.dot(q, ref[c, :HEAD, b : b + bk], preferred_element_type=jnp.float32)
                weights = jnp.exp2(scores).astype(jnp.bfloat16)
                at = (n * blocks + c) * nk + b
                values = v1[at : at + bk, :]
                acc = acc + jnp.dot(weights, values, preferred_element_type=jnp.float32)
        return acc

    if acc_refs:
        acc = acc_refs[0][...]
    else:
        acc = jnp.zeros((bq, 2 * HEAD), jnp.float32)
    for c in range(blocks):
        acc = body(c, acc)
    if last:
        halves = (acc / pltpu.roll(acc, HEAD, 1)).reshape(bq // 64, 2, 32, 2 * HEAD)
        left, right = halves[:, 0], halves[:, 1]
        right = pltpu.roll(right.reshape(bq // 2, 2 * HEAD), HEAD, 1).reshape(left.shape)
        lane = lax.broadcasted_iota(jnp.int32, left.shape, 2)
        packed = jnp.where(lane < HEAD, left, right).astype(jnp.bfloat16)
        half = packed.shape[0] // 2
        yh = ids_ref[3]
        o_ref[pl.ds(yh * half, half)] = packed[:half]
        o_ref[pl.ds(half - yh * half, half)] = packed[half:]
    else:
        o_ref[...] = acc


def attend(ids, q, kv, acc=None, last=False):
    n = q.shape[0]
    bq = n // CORE
    keys = 2 * kv[0].shape[0] * kv[0].shape[2]
    rows = lambda w: pl.BlockSpec((bq, w), lambda i, s: (i, 0))
    if last:
        out_spec = pl.BlockSpec((bq // 64, 32, 2 * HEAD), lambda i, s: ((i + s[1]) % CORE, 0, 0))
        out_shape = jax.ShapeDtypeStruct((n // 64, 32, 2 * HEAD), jnp.bfloat16)
    else:
        out_spec = rows(2 * HEAD)
        out_shape = jax.ShapeDtypeStruct((n, 2 * HEAD), jnp.float32)
    return pl.pallas_call(
        functools.partial(attend_kernel, last),
        grid_spec=pltpu.PrefetchScalarGridSpec(
            num_scalar_prefetch=1,
            grid=(CORE,),
            in_specs=[rows(HEAD)]
            + [pl.BlockSpec(a.shape, lambda i, s: (0, 0, 0)) for a in kv]
            + ([rows(2 * HEAD)] if acc is not None else []),
            out_specs=out_spec,
            scratch_shapes=[pltpu.VMEM((keys, 2 * HEAD), jnp.bfloat16)],
        ),
        out_shape=out_shape,
        compiler_params=pltpu.CompilerParams(vmem_limit_bytes=40 * 2**20),
        cost_estimate=pl.CostEstimate(
            flops=12 * n * keys * HEAD, bytes_accessed=4 * 2**20, transcendentals=n * keys
        ),
    )(ids, q, *kv, *([acc] if acc is not None else []))


def ring_z(own, beside, parts=1):
    z = lax.axis_index("z")
    rows, members, cols, width = own.shape
    size = rows // parts
    forward = [(i, (i + 1) % Z) for i in range(Z)]
    backward = [(target, source) for source, target in forward]
    out = jnp.zeros((rows, members, Z * cols, width), own.dtype)

    def place(out, shard, part, at):
        return lax.dynamic_update_slice(out, shard, (part * size, 0, (at % Z) * cols, 0))

    out = place(out, own, 0, z)
    ups = [own[p * size : (p + 1) * size] for p in range(parts)]
    downs = list(ups)
    for step in range(1, Z // 2 + 1):
        for p in range(parts):
            ups[p] = lax.ppermute(ups[p], "z", forward)
            if step < Z // 2:
                downs[p] = lax.ppermute(downs[p], "z", backward)
        if step == 2:
            ups, downs, beside = lax.optimization_barrier((ups, downs, beside))
        for p in range(parts):
            out = place(out, ups[p], p, z - step + Z)
            if step < Z // 2:
                out = place(out, downs[p], p, z + step)
    return out, beside


def project_kernel(ids_ref, x_ref, own_ref, other_ref, gain_ref, *out_refs):
    core = ids_ref[1]
    for rel_core in range(2):
        member = core if rel_core == 0 else 1 - core
        x = x_ref[:, member].reshape(-1, x_ref.shape[3])
        for rel_head, w in enumerate((own_ref[...], other_ref[: 3 * HEAD])):
            out = lax.dot_general(
                w, x, (((1,), (1,)), ((), ())), preferred_element_type=jnp.float32
            )
            out_ref = out_refs[2 * rel_core + rel_head]
            for kind in range(2):
                part = out[kind * HEAD : (kind + 1) * HEAD]
                mean = jnp.mean(part * part, axis=0, keepdims=True)
                part = part * lax.rsqrt(mean + head_epsilon) * gain_ref[rel_head, kind]
                if kind == 0:
                    part = part * (LOG2E / 8.0)
                out_ref[kind * HEAD : (kind + 1) * HEAD, :] = part.astype(jnp.bfloat16)
            out_ref[2 * HEAD :, :] = out[2 * HEAD :].astype(jnp.bfloat16)


def project(x, own, other, gains, ids):
    tokens = x.shape[0] * x.shape[2]
    whole = lambda a: pl.BlockSpec(a.shape, lambda i, s: (0,) * a.ndim)
    out = jax.ShapeDtypeStruct((3 * HEAD, tokens), jnp.bfloat16)
    return pl.pallas_call(
        project_kernel,
        grid_spec=pltpu.PrefetchScalarGridSpec(
            num_scalar_prefetch=1,
            grid=(1,),
            in_specs=[whole(x), whole(own), whole(other), whole(gains)],
            out_specs=[whole(out)] * 4,
        ),
        out_shape=[out] * 4,
        compiler_params=pltpu.CompilerParams(vmem_limit_bytes=32 * 2**20),
        cost_estimate=pl.CostEstimate(flops=3 * 10**9, bytes_accessed=4 * 2**20, transcendentals=0),
    )(ids, x, own, other, gains)


def mlp_kernel(ids_ref, x_ref, tok_ref, gu_ref, down_ref, some_ref, rest_ref, o_ref, acc):
    rows, members, cols, width = x_ref.shape
    units = down_ref.shape[0] // 2
    x = x_ref[...].reshape(-1, width)
    contract = (((1,), (1,)), ((), ()))
    other = []
    for n in range(3):
        rows_n = slice(n * units, (n + 1) * units)
        other.append(jnp.concatenate([some_ref[rows_n], rest_ref[rows_n]], 0))
    total = None
    for gate_w, up_w, down_w in ((gu_ref[0], gu_ref[1], down_ref[...]), other):
        gate = lax.dot_general(x, gate_w, contract, preferred_element_type=jnp.float32)
        up = lax.dot_general(x, up_w, contract, preferred_element_type=jnp.float32)
        hidden = (gate / (1.0 + jnp.exp(-gate)) * up).astype(jnp.bfloat16)
        term = jnp.dot(hidden, down_w, preferred_element_type=jnp.float32)
        total = term if total is None else total + term
    acc[...] = total.reshape(acc.shape)
    at = pl.multiple_of(ids_ref[2] * 8, 8)
    acc[:, :, pl.ds(at, 8), :] += tok_ref[...].astype(jnp.float32)
    o_ref[...] = acc[...].astype(jnp.bfloat16)


def mlp(x, tokens, gu, down, some, rest, ids, rows=4):
    whole = lambda a: pl.BlockSpec(a.shape, lambda i, s: (0,) * a.ndim)
    block = lambda a: pl.BlockSpec((rows,) + a.shape[1:], lambda i, s: (i, 0, 0, 0))
    return pl.pallas_call(
        mlp_kernel,
        grid_spec=pltpu.PrefetchScalarGridSpec(
            num_scalar_prefetch=1,
            grid=(x.shape[0] // rows,),
            in_specs=[block(x), block(tokens)] + [whole(a) for a in (gu, down, some, rest)],
            out_specs=block(x),
            scratch_shapes=[pltpu.VMEM((rows,) + x.shape[1:], jnp.float32)],
        ),
        out_shape=jax.ShapeDtypeStruct(x.shape, jnp.bfloat16),
        compiler_params=pltpu.CompilerParams(vmem_limit_bytes=32 * 2**20),
        cost_estimate=pl.CostEstimate(flops=6 * 10**9, bytes_accessed=8 * 2**20, transcendentals=0),
    )(ids, x, tokens, gu, down, some, rest)


def shards(
    fields,
    embed_weight,
    embed_bias,
    pos_embed,
    member_ids,
    member_table,
    norm_gain,
    w_qkv,
    query_gain,
    key_gain,
    w_gate_up,
    w_out,
    w_down,
):
    f32, bf16 = jnp.float32, jnp.bfloat16
    width = embed_weight.shape[3]
    yl = lax.axis_index("yl")
    yh = lax.axis_index("yh")
    core = lax.axis_index("core")

    gains = jnp.concatenate([query_gain, key_gain], 0)
    coarse = lax.reduce_precision(gains, 8, 7)
    middle = lax.reduce_precision(gains - coarse, 8, 7)
    fine = gains - coarse - middle
    terms = jnp.stack([coarse, middle, fine], 0).astype(bf16).reshape(1, 6 * HEAD)
    terms = jnp.pad(terms, ((0, 15), (0, width - 6 * HEAD)))
    ids = jnp.stack([yl, core, lax.axis_index("z"), yh]).astype(jnp.int32)

    f = jnp.transpose(fields, (0, 2, 3, 1))
    row, low, high = halo(f, ids, yl)
    part = embed(f, row, low, high, embed_weight, pos_embed, ids)
    part = lax.all_to_all(part, ("yh", "yl"), 0, 0, tiled=True)
    part, terms, w_qkv, w_gate_up, w_down, w_out = lax.optimization_barrier(
        (part, terms, w_qkv, w_gate_up, w_down, w_out)
    )
    w_out_half = lax.all_gather(w_out, "z", axis=0, tiled=True)
    qkv_other = other_half_weights(jnp.concatenate([w_qkv.reshape(-1, width), terms], 0))
    units = w_down.shape[0] // 2
    some_gu = lax.dynamic_slice_in_dim(w_gate_up, core * units, units, 1)
    some_down = lax.dynamic_slice_in_dim(w_down, core * units, units, 0)
    mlp_other = other_half_weights(
        jnp.concatenate([some_gu.reshape(-1, width), some_down], 0)
    )
    terms = qkv_other[-16:, : 6 * HEAD][0].astype(f32).reshape(3, 2, HEAD)
    gains_other = terms[0] + terms[1] + terms[2]
    gain_both = jnp.stack([gains, gains_other], 0)[..., None]
    part = part.reshape(YH, YL, 4, 2, 8, width).astype(f32)
    embedded = jnp.transpose(part[:, 0] + part[:, 1], (1, 0, 2, 3, 4)).reshape(8, 2, 8, width)
    one_hot = (
        member_ids[:, None] == jnp.arange(member_table.shape[0], dtype=jnp.int32)[None, :]
    ).astype(bf16)
    member_vecs = jnp.dot(one_hot, member_table, preferred_element_type=f32)
    tokens = (
        embedded
        + embed_bias.astype(f32)
        + member_vecs[None, :, None, :]
    ).astype(bf16)
    residual = tokens.astype(f32)
    average = jnp.mean(residual, axis=-1, keepdims=True)
    centered = residual - average
    variance = jnp.mean(centered * centered, axis=-1, keepdims=True)
    normed = (centered * lax.rsqrt(variance + layer_epsilon) * norm_gain).astype(bf16)

    normed_all, qkv_other = ring_z(normed, qkv_other)
    normed_all, mlp_other = lax.optimization_barrier((normed_all, mlp_other))

    mine, mine_yh, theirs, theirs_yh = project(
        normed_all, w_qkv.reshape(3 * HEAD, width), qkv_other, gain_both, ids
    )
    pair = ("core", "yh")
    got_core = lax.ppermute(theirs, pair, [(0, 2), (2, 0), (1, 3), (3, 1)])
    got_yh = lax.ppermute(mine_yh, pair, [(0, 1), (1, 0), (2, 3), (3, 2)])
    got_both = lax.ppermute(theirs_yh, pair, [(0, 3), (3, 0), (1, 2), (2, 1)])

    mlp_rest = lax.ppermute(mlp_other, "core", [(0, 1), (1, 0)])
    update = mlp(normed_all, tokens, w_gate_up, w_down, mlp_other, mlp_rest, ids)
    got_core, got_yh, got_both, update = lax.optimization_barrier(
        (got_core, got_yh, got_both, update)
    )
    summed = lax.psum_scatter(update, "z", scatter_dimension=0, tiled=True)[0]
    first = jnp.stack([mine[HEAD:], got_yh[HEAD:]], 0)
    second = jnp.stack([got_core[HEAD:], got_both[HEAD:]], 0)
    q = jnp.stack([a[:HEAD] for a in (mine, got_yh, got_core, got_both)], 0)
    q = jnp.transpose(q, (0, 2, 1)).reshape(-1, HEAD)

    x_up = [(i, (i + 1) % X) for i in range(X)]
    x_down = [(target, source) for source, target in x_up]
    near = [lax.ppermute(first, "x", x_up), lax.ppermute(second, "x", x_down)]
    late = [lax.ppermute(second, "x", x_up), lax.ppermute(first, "x", x_down)]
    far = [lax.ppermute(near[0], "x", x_up), lax.ppermute(near[1], "x", x_down)]

    acc = attend(ids, q, (first, second))
    acc, w_out_half = lax.optimization_barrier((acc, w_out_half))
    w_out_other = other_half_weights(w_out_half)
    acc = attend(ids, q, near, acc)
    acc = attend(ids, q, late, acc)
    attended = attend(ids, q, far, acc, last=True)
    attended = lax.all_to_all(attended, ("core", "yh", "z"), 0, 0, tiled=True)
    attended = attended.reshape(CORE, YH, Z, 32, 2, HEAD)
    attended = jnp.transpose(attended, (0, 4, 3, 1, 2, 5)).reshape(CORE * 64, YH * Z * HEAD)
    half = Z * HEAD
    own_cols = lax.dynamic_slice_in_dim(attended, yh * half, half, 1)
    other_cols = lax.dynamic_slice_in_dim(attended, half - yh * half, half, 1)
    mixed = jnp.dot(own_cols, w_out_half, preferred_element_type=f32)
    mixed = mixed + jnp.dot(other_cols, w_out_other, preferred_element_type=f32)
    mixed = mixed.reshape(2, 64, width)
    return (summed.astype(f32) + mixed).astype(bf16)


def solution(mesh):
    chips = Mesh(mesh.devices.reshape(X, CORE, YH, Z, YL), ("x", "core", "yh", "z", "yl"))
    return jax.shard_map(
        shards,
        mesh=chips,
        in_specs=(
            P(None, None, LAT, LON),
            P("yl", None, None, None),
            P(),
            P(LAT, LON, None),
            P("yl"),
            P(),
            P(),
            P(None, LON, None),
            P(LON, None),
            P(LON, None),
            P(None, LON, None),
            P(LON, None),
            P(LON, None),
        ),
        out_specs=P("yl", LAT + LON, None),
        check_vma=False,
    )
```

```python
import functools

import jax
import jax.numpy as jnp
from jax import lax
from jax.experimental import pallas as pl
from jax.experimental.pallas import tpu as pltpu
from jax.sharding import Mesh, PartitionSpec as P

PATCH = 8
layer_epsilon = 1e-05
head_epsilon = 1e-06
LOG2E = 1.4426950408889634
HEAD = 64

X, CORE, YH, Z, YL = 4, 2, 2, 8, 2
LAT = ("x", "core")
LON = ("yh", "z")


def other_half_weights(array):
    return lax.ppermute(array, ("yh", "yl"), [(0, 3), (3, 0), (1, 2), (2, 1)])


def edges_kernel(s_ref, top_ref, left_ref, right_ref, row_ref, low_ref, high_ref, wide):
    row_ref[...] = top_ref[:, 0]
    members, rows, cols, channels = right_ref.shape
    wide[..., :channels] = right_ref[...].reshape(wide.shape[0], cols, channels).astype(jnp.float32)
    low = wide[:, cols - 1, :channels]
    low_ref[...] = low.reshape(low_ref.shape).astype(jnp.bfloat16)
    wide[..., :channels] = left_ref[...].reshape(wide.shape[0], cols, channels).astype(jnp.float32)
    high = wide[:, 0, :channels]
    high_ref[...] = high.reshape(high_ref.shape).astype(jnp.bfloat16)


def edges(f, ids):
    members, rows, cols, channels = f.shape
    column = (members, rows, 16, channels)
    line = jax.ShapeDtypeStruct((members, rows, channels), f.dtype)
    whole = pl.BlockSpec((members, rows, channels), lambda i, s: (0, 0, 0))
    return pl.pallas_call(
        edges_kernel,
        grid_spec=pltpu.PrefetchScalarGridSpec(
            num_scalar_prefetch=1,
            grid=(1,),
            in_specs=[
                pl.BlockSpec(
                    (members, 1, cols, channels), lambda i, s: (0, (1 - s[0]) * (rows - 1), 0, 0)
                ),
                pl.BlockSpec(column, lambda i, s: (0, 0, 0, 0)),
                pl.BlockSpec(column, lambda i, s: (0, 0, cols // 16 - 1, 0)),
            ],
            out_specs=[whole] * 3,
            scratch_shapes=[pltpu.VMEM((members * rows, 16, 128), jnp.float32)],
        ),
        out_shape=[line] * 3,
        compiler_params=pltpu.CompilerParams(vmem_limit_bytes=40 * 2**20),
    )(ids, f, f, f)


def halo(f, ids, section):
    lats, lons = X * CORE, YH * Z
    row, low, high = edges(f, ids)
    to_lat = [(2 * i, 2 * i + 2) for i in range(lats - 1)]
    to_lat += [(2 * i + 1, 2 * i - 1) for i in range(1, lats)]
    forward = [(i, (i + 1) % lons) for i in range(lons)]
    backward = [(target, source) for source, target in forward]
    row = lax.ppermute(row, LAT + ("yl",), to_lat)

    def column(edge, corner, pairs):
        edge = jnp.concatenate([edge, corner[:, None]], 1)
        edge = lax.ppermute(edge, LON, pairs)
        edge = jnp.concatenate([edge[:, -1:], edge, jnp.zeros_like(edge[:, :3])], 1)
        edge = lax.dynamic_slice_in_dim(edge, section * 5, 64, 1)
        edge = edge.reshape(2, 2, 2, 4, 8, edge.shape[-1])[:, :, :, :, :5].astype(jnp.float32)
        return jnp.transpose(edge, (4, 2, 0, 3, 1, 5)).reshape(5, 32, edge.shape[-1])

    return row, column(low, row[:, -1], forward), column(high, row[:, 0], backward)


def embed_kernel(
    ids_ref, f_ref, row_ref, low_ref, high_ref, w_ref, w2_ref, pos_ref, out_ref, xf, rhs, acc
):
    step = pl.program_id(0)
    section = ids_ref[0]
    channels = f_ref.shape[4]
    offset = step - 1 + 5 * section
    shift = jnp.where(offset < 0, -1, jnp.where(offset > 7, 1, 0))

    @pl.when(step == 0)
    def _():
        xf[...] = jnp.zeros_like(xf)
        rhs[...] = jnp.zeros_like(rhs)
        acc[...] = jnp.zeros_like(acc)

    for slot in range(32):
        patch = slot // 16 * 4 + slot // 2 % 4
        member = slot // 8 % 2 * 2 + slot % 2
        at = patch + shift
        value = f_ref[member, jnp.clip(at, 0, 7), 0]
        if patch in (0, 7):
            value = jnp.where((at < 0) | (at > 7), row_ref[member], value)
        xf[slot, 8:72, :channels] = value.astype(jnp.float32)
        xf[slot, 7:8, :channels] = low_ref[0, slot : slot + 1]
        xf[slot, 72:73, :channels] = high_ref[0, slot : slot + 1]
    half = w_ref.shape[1]
    columns = []
    for b in range(2 * half):
        rhs[b * 128 : b * 128 + channels, :] = (w_ref if b < half else w2_ref)[0, b % half]
        column = xf[:, pl.ds(7 + b, 8, stride=8), :]
        columns.append(column.reshape(256, 128).astype(jnp.bfloat16))
    lhs = jnp.concatenate(columns, 1)
    acc[...] += jnp.dot(lhs, rhs[...], preferred_element_type=jnp.float32)

    @pl.when(step == pl.num_programs(0) - 1)
    def _():
        first = jnp.where(section == 0, 1.0, 0.0)
        for slot in range(32):
            patch = slot // 16 * 4 + slot // 2 % 4
            rows = slice(8 * slot, 8 * slot + 8)
            acc[rows, :] += first * pos_ref[patch].astype(jnp.float32)
        out_ref[...] = acc[...].astype(jnp.bfloat16)


def embed(f, row, low, high, weight, pos, ids):
    taps, cols, channels, width = weight.shape
    members, rows, wide, _ = f.shape
    whole = lambda n: (lambda i, s: (0,) * n)
    return pl.pallas_call(
        embed_kernel,
        grid_spec=pltpu.PrefetchScalarGridSpec(
            num_scalar_prefetch=1,
            grid=(taps,),
            in_specs=[
                pl.BlockSpec(
                    (members, 8, 1, wide, channels),
                    lambda i, s: (0, 0, (i + 7 + 5 * s[0]) % 8, 0, 0),
                ),
                pl.BlockSpec(row.shape, whole(3)),
                pl.BlockSpec((1, 32, channels), lambda i, s: (i, 0, 0)),
                pl.BlockSpec((1, 32, channels), lambda i, s: (i, 0, 0)),
                pl.BlockSpec((1, cols // 2, channels, width), lambda i, s: (i, 0, 0, 0)),
                pl.BlockSpec((1, cols // 2, channels, width), lambda i, s: (i, 1, 0, 0)),
                pl.BlockSpec(pos.shape, whole(3)),
            ],
            out_specs=pl.BlockSpec((256, width), whole(2)),
            scratch_shapes=[
                pltpu.VMEM((32, 80, 128), jnp.float32),
                pltpu.VMEM((cols * 128, width), jnp.bfloat16),
                pltpu.VMEM((256, width), jnp.float32),
            ],
        ),
        out_shape=jax.ShapeDtypeStruct((256, width), jnp.bfloat16),
        compiler_params=pltpu.CompilerParams(vmem_limit_bytes=52 * 2**20),
        cost_estimate=pl.CostEstimate(
            flops=8 * 10**9, bytes_accessed=12 * 2**20, transcendentals=0
        ),
    )(ids, f.reshape(members, 8, rows // 8, wide, channels), row, low, high, weight, weight, pos)


def attend_kernel(last, ids_ref, q_ref, kv_ref, kv2_ref, *refs):
    acc_refs, o_ref, v1 = refs[:-2], refs[-2], refs[-1]
    blocks, _, nk = kv_ref.shape
    bq = q_ref.shape[0]
    bk = 256

    @pl.when(pl.program_id(0) == 0)
    def _():
        for c in range(2 * blocks):
            rows = (kv_ref if c < blocks else kv2_ref)[c % blocks, HEAD:, :]
            stacked = jnp.concatenate([rows, jnp.ones_like(rows)], 0)
            v1[pl.ds(c * nk, nk), :] = stacked.T

    q = q_ref[...]

    def body(c, acc):
        for n, ref in enumerate((kv_ref, kv2_ref)):
            for b in range(0, nk, bk):
                scores = jnp.dot(q, ref[c, :HEAD, b : b + bk], preferred_element_type=jnp.float32)
                weights = jnp.exp2(scores).astype(jnp.bfloat16)
                at = (n * blocks + c) * nk + b
                values = v1[at : at + bk, :]
                acc = acc + jnp.dot(weights, values, preferred_element_type=jnp.float32)
        return acc

    if acc_refs:
        acc = acc_refs[0][...]
    else:
        acc = jnp.zeros((bq, 2 * HEAD), jnp.float32)
    for c in range(blocks):
        acc = body(c, acc)
    if last:
        halves = (acc / pltpu.roll(acc, HEAD, 1)).reshape(bq // 64, 2, 32, 2 * HEAD)
        left, right = halves[:, 0], halves[:, 1]
        right = pltpu.roll(right.reshape(bq // 2, 2 * HEAD), HEAD, 1).reshape(left.shape)
        lane = lax.broadcasted_iota(jnp.int32, left.shape, 2)
        packed = jnp.where(lane < HEAD, left, right).astype(jnp.bfloat16)
        half = packed.shape[0] // 2
        yh = ids_ref[3]
        o_ref[pl.ds(yh * half, half)] = packed[:half]
        o_ref[pl.ds(half - yh * half, half)] = packed[half:]
    else:
        o_ref[...] = acc


def attend(ids, q, kv, acc=None, last=False):
    n = q.shape[0]
    bq = n // CORE
    keys = 2 * kv[0].shape[0] * kv[0].shape[2]
    rows = lambda w: pl.BlockSpec((bq, w), lambda i, s: (i, 0))
    if last:
        out_spec = pl.BlockSpec((bq // 64, 32, 2 * HEAD), lambda i, s: ((i + s[1]) % CORE, 0, 0))
        out_shape = jax.ShapeDtypeStruct((n // 64, 32, 2 * HEAD), jnp.bfloat16)
    else:
        out_spec = rows(2 * HEAD)
        out_shape = jax.ShapeDtypeStruct((n, 2 * HEAD), jnp.float32)
    return pl.pallas_call(
        functools.partial(attend_kernel, last),
        grid_spec=pltpu.PrefetchScalarGridSpec(
            num_scalar_prefetch=1,
            grid=(CORE,),
            in_specs=[rows(HEAD)]
            + [pl.BlockSpec(a.shape, lambda i, s: (0, 0, 0)) for a in kv]
            + ([rows(2 * HEAD)] if acc is not None else []),
            out_specs=out_spec,
            scratch_shapes=[pltpu.VMEM((keys, 2 * HEAD), jnp.bfloat16)],
        ),
        out_shape=out_shape,
        compiler_params=pltpu.CompilerParams(vmem_limit_bytes=40 * 2**20),
        cost_estimate=pl.CostEstimate(
            flops=12 * n * keys * HEAD, bytes_accessed=4 * 2**20, transcendentals=n * keys
        ),
    )(ids, q, *kv, *([acc] if acc is not None else []))


def ring_z(own, beside, parts=1):
    z = lax.axis_index("z")
    rows, members, cols, width = own.shape
    size = rows // parts
    forward = [(i, (i + 1) % Z) for i in range(Z)]
    backward = [(target, source) for source, target in forward]
    out = jnp.zeros((rows, members, Z * cols, width), own.dtype)

    def place(out, shard, part, at):
        return lax.dynamic_update_slice(out, shard, (part * size, 0, (at % Z) * cols, 0))

    out = place(out, own, 0, z)
    ups = [own[p * size : (p + 1) * size] for p in range(parts)]
    downs = list(ups)
    for step in range(1, Z // 2):
        for p in range(parts):
            ups[p] = lax.ppermute(ups[p], "z", forward)
            downs[p] = lax.ppermute(downs[p], "z", backward)
        if step == 2:
            ups, downs, beside = lax.optimization_barrier((ups, downs, beside))
        for p in range(parts):
            out = place(out, ups[p], p, z - step + Z)
            out = place(out, downs[p], p, z + step)
    far = size // 2
    for p in range(parts):
        up = lax.ppermute(ups[p][:far], "z", forward)
        down = lax.ppermute(downs[p][far:], "z", backward)
        at = ((z + Z // 2) % Z) * cols
        out = lax.dynamic_update_slice(out, up, (p * size, 0, at, 0))
        out = lax.dynamic_update_slice(out, down, (p * size + far, 0, at, 0))
    return out, beside


def project_kernel(ids_ref, x_ref, own_ref, other_ref, gain_ref, *out_refs):
    core = ids_ref[1]
    for rel_core in range(2):
        member = core if rel_core == 0 else 1 - core
        x = x_ref[:, member].reshape(-1, x_ref.shape[3])
        for rel_head, w in enumerate((own_ref[...], other_ref[: 3 * HEAD])):
            out = lax.dot_general(
                w, x, (((1,), (1,)), ((), ())), preferred_element_type=jnp.float32
            )
            out_ref = out_refs[2 * rel_core + rel_head]
            for kind in range(2):
                part = out[kind * HEAD : (kind + 1) * HEAD]
                mean = jnp.mean(part * part, axis=0, keepdims=True)
                part = part * lax.rsqrt(mean + head_epsilon) * gain_ref[rel_head, kind]
                if kind == 0:
                    part = part * (LOG2E / 8.0)
                out_ref[kind * HEAD : (kind + 1) * HEAD, :] = part.astype(jnp.bfloat16)
            out_ref[2 * HEAD :, :] = out[2 * HEAD :].astype(jnp.bfloat16)


def project(x, own, other, gains, ids):
    tokens = x.shape[0] * x.shape[2]
    whole = lambda a: pl.BlockSpec(a.shape, lambda i, s: (0,) * a.ndim)
    out = jax.ShapeDtypeStruct((3 * HEAD, tokens), jnp.bfloat16)
    return pl.pallas_call(
        project_kernel,
        grid_spec=pltpu.PrefetchScalarGridSpec(
            num_scalar_prefetch=1,
            grid=(1,),
            in_specs=[whole(x), whole(own), whole(other), whole(gains)],
            out_specs=[whole(out)] * 4,
        ),
        out_shape=[out] * 4,
        compiler_params=pltpu.CompilerParams(vmem_limit_bytes=32 * 2**20),
        cost_estimate=pl.CostEstimate(flops=3 * 10**9, bytes_accessed=4 * 2**20, transcendentals=0),
    )(ids, x, own, other, gains)


def mlp_kernel(ids_ref, x_ref, tok_ref, gu_ref, down_ref, some_ref, rest_ref, o_ref, acc):
    rows, members, cols, width = x_ref.shape
    units = down_ref.shape[0] // 2
    x = x_ref[...].reshape(-1, width)
    contract = (((1,), (1,)), ((), ()))
    other = []
    for n in range(3):
        rows_n = slice(n * units, (n + 1) * units)
        other.append(jnp.concatenate([some_ref[rows_n], rest_ref[rows_n]], 0))
    total = None
    for gate_w, up_w, down_w in ((gu_ref[0], gu_ref[1], down_ref[...]), other):
        gate = lax.dot_general(x, gate_w, contract, preferred_element_type=jnp.float32)
        up = lax.dot_general(x, up_w, contract, preferred_element_type=jnp.float32)
        hidden = (gate / (1.0 + jnp.exp(-gate)) * up).astype(jnp.bfloat16)
        term = jnp.dot(hidden, down_w, preferred_element_type=jnp.float32)
        total = term if total is None else total + term
    acc[...] = total.reshape(acc.shape)
    at = pl.multiple_of(ids_ref[2] * 8, 8)
    acc[:, :, pl.ds(at, 8), :] += tok_ref[...].astype(jnp.float32)
    o_ref[...] = acc[...].astype(jnp.bfloat16)


def mlp(x, tokens, gu, down, some, rest, ids, rows=4):
    whole = lambda a: pl.BlockSpec(a.shape, lambda i, s: (0,) * a.ndim)
    block = lambda a: pl.BlockSpec((rows,) + a.shape[1:], lambda i, s: (i, 0, 0, 0))
    return pl.pallas_call(
        mlp_kernel,
        grid_spec=pltpu.PrefetchScalarGridSpec(
            num_scalar_prefetch=1,
            grid=(x.shape[0] // rows,),
            in_specs=[block(x), block(tokens)] + [whole(a) for a in (gu, down, some, rest)],
            out_specs=block(x),
            scratch_shapes=[pltpu.VMEM((rows,) + x.shape[1:], jnp.float32)],
        ),
        out_shape=jax.ShapeDtypeStruct(x.shape, jnp.bfloat16),
        compiler_params=pltpu.CompilerParams(vmem_limit_bytes=32 * 2**20),
        cost_estimate=pl.CostEstimate(flops=6 * 10**9, bytes_accessed=8 * 2**20, transcendentals=0),
    )(ids, x, tokens, gu, down, some, rest)


def shards(
    fields,
    embed_weight,
    embed_bias,
    pos_embed,
    member_ids,
    member_table,
    norm_gain,
    w_qkv,
    query_gain,
    key_gain,
    w_gate_up,
    w_out,
    w_down,
):
    f32, bf16 = jnp.float32, jnp.bfloat16
    width = embed_weight.shape[3]
    yl = lax.axis_index("yl")
    yh = lax.axis_index("yh")
    core = lax.axis_index("core")

    gains = jnp.concatenate([query_gain, key_gain], 0)
    coarse = lax.reduce_precision(gains, 8, 7)
    middle = lax.reduce_precision(gains - coarse, 8, 7)
    fine = gains - coarse - middle
    terms = jnp.stack([coarse, middle, fine], 0).astype(bf16).reshape(1, 6 * HEAD)
    terms = jnp.pad(terms, ((0, 15), (0, width - 6 * HEAD)))
    ids = jnp.stack([yl, core, lax.axis_index("z"), yh]).astype(jnp.int32)

    f = jnp.transpose(fields, (0, 2, 3, 1))
    row, low, high = halo(f, ids, yl)
    part = embed(f, row, low, high, embed_weight, pos_embed, ids)
    part = lax.all_to_all(part, ("yh", "yl"), 0, 0, tiled=True)
    part, terms, w_qkv, w_gate_up, w_down, w_out = lax.optimization_barrier(
        (part, terms, w_qkv, w_gate_up, w_down, w_out)
    )
    w_out_half = lax.all_gather(w_out, "z", axis=0, tiled=True)
    qkv_other = other_half_weights(jnp.concatenate([w_qkv.reshape(-1, width), terms], 0))
    units = w_down.shape[0] // 2
    some_gu = lax.dynamic_slice_in_dim(w_gate_up, core * units, units, 1)
    some_down = lax.dynamic_slice_in_dim(w_down, core * units, units, 0)
    mlp_other = other_half_weights(
        jnp.concatenate([some_gu.reshape(-1, width), some_down], 0)
    )
    terms = qkv_other[-16:, : 6 * HEAD][0].astype(f32).reshape(3, 2, HEAD)
    gains_other = terms[0] + terms[1] + terms[2]
    gain_both = jnp.stack([gains, gains_other], 0)[..., None]
    part = part.reshape(YH, YL, 4, 2, 8, width).astype(f32)
    embedded = jnp.transpose(part[:, 0] + part[:, 1], (1, 0, 2, 3, 4)).reshape(8, 2, 8, width)
    one_hot = (
        member_ids[:, None] == jnp.arange(member_table.shape[0], dtype=jnp.int32)[None, :]
    ).astype(bf16)
    member_vecs = jnp.dot(one_hot, member_table, preferred_element_type=f32)
    tokens = (
        embedded
        + embed_bias.astype(f32)
        + member_vecs[None, :, None, :]
    ).astype(bf16)
    residual = tokens.astype(f32)
    average = jnp.mean(residual, axis=-1, keepdims=True)
    centered = residual - average
    variance = jnp.mean(centered * centered, axis=-1, keepdims=True)
    normed = (centered * lax.rsqrt(variance + layer_epsilon) * norm_gain).astype(bf16)

    normed_all, qkv_other = ring_z(normed, qkv_other)
    normed_all, mlp_other = lax.optimization_barrier((normed_all, mlp_other))

    mine, mine_yh, theirs, theirs_yh = project(
        normed_all, w_qkv.reshape(3 * HEAD, width), qkv_other, gain_both, ids
    )
    pair = ("core", "yh")
    got_core = lax.ppermute(theirs, pair, [(0, 2), (2, 0), (1, 3), (3, 1)])
    got_yh = lax.ppermute(mine_yh, pair, [(0, 1), (1, 0), (2, 3), (3, 2)])
    got_both = lax.ppermute(theirs_yh, pair, [(0, 3), (3, 0), (1, 2), (2, 1)])

    mlp_rest = lax.ppermute(mlp_other, "core", [(0, 1), (1, 0)])
    update = mlp(normed_all, tokens, w_gate_up, w_down, mlp_other, mlp_rest, ids)
    got_core, got_yh, got_both, update = lax.optimization_barrier(
        (got_core, got_yh, got_both, update)
    )
    summed = lax.psum_scatter(update, "z", scatter_dimension=0, tiled=True)[0]
    first = jnp.stack([mine[HEAD:], got_yh[HEAD:]], 0)
    second = jnp.stack([got_core[HEAD:], got_both[HEAD:]], 0)
    q = jnp.stack([a[:HEAD] for a in (mine, got_yh, got_core, got_both)], 0)
    q = jnp.transpose(q, (0, 2, 1)).reshape(-1, HEAD)

    x_up = [(i, (i + 1) % X) for i in range(X)]
    x_down = [(target, source) for source, target in x_up]
    near = [lax.ppermute(first, "x", x_up), lax.ppermute(second, "x", x_down)]
    late = [lax.ppermute(second, "x", x_up), lax.ppermute(first, "x", x_down)]
    far = [lax.ppermute(near[0], "x", x_up), lax.ppermute(near[1], "x", x_down)]

    acc = attend(ids, q, (first, second))
    then_ids, w_out_half = lax.optimization_barrier((ids, w_out_half))
    w_out_other = other_half_weights(w_out_half)
    acc = attend(then_ids, q, near, acc)
    acc = attend(ids, q, late, acc)
    attended = attend(ids, q, far, acc, last=True)
    attended = lax.all_to_all(attended, ("core", "yh", "z"), 0, 0, tiled=True)
    attended = attended.reshape(CORE, YH, Z, 32, 2, HEAD)
    attended = jnp.transpose(attended, (0, 4, 3, 1, 2, 5)).reshape(CORE * 64, YH * Z * HEAD)
    half = Z * HEAD
    own_cols = lax.dynamic_slice_in_dim(attended, yh * half, half, 1)
    other_cols = lax.dynamic_slice_in_dim(attended, half - yh * half, half, 1)
    mixed = jnp.dot(own_cols, w_out_half, preferred_element_type=f32)
    mixed = mixed + jnp.dot(other_cols, w_out_other, preferred_element_type=f32)
    mixed = mixed.reshape(2, 64, width)
    return (summed.astype(f32) + mixed).astype(bf16)


def solution(mesh):
    chips = Mesh(mesh.devices.reshape(X, CORE, YH, Z, YL), ("x", "core", "yh", "z", "yl"))
    return jax.shard_map(
        shards,
        mesh=chips,
        in_specs=(
            P(None, None, LAT, LON),
            P("yl", None, None, None),
            P(),
            P(LAT, LON, None),
            P("yl"),
            P(),
            P(),
            P(None, LON, None),
            P(LON, None),
            P(LON, None),
            P(None, LON, None),
            P(LON, None),
            P(LON, None),
        ),
        out_specs=P("yl", LAT + LON, None),
        check_vma=False,
    )
```
